32 devices in a mesh: order: 4 (over z), heads: 2 (over core), seq: 4 (over y, x).
Axes of the slice: x: 2, y: 2, z: 4, core: 2. Of those that a mesh axis runs over, the one named last changes fastest.
Arguments:
- tokens: bfloat16 [4, 2048, 1024], P('seq', 'order'), may hold values from -6 to 6
- cotangent: bfloat16 [4, 2048, 1024], P('seq', 'order'), may hold values from -1 to 1
- node_order: int32 [4, 2048], P('seq', 'order'), may hold values from 0 to 2047, as said below
- decays: float32 [4, 2048, 32], P('seq', 'order', 'heads'), may hold values from 0.4 to 1, as said below
- w_inner: bfloat16 [1024, 2048], P(None, 'heads'), may hold values from -0.1875 to 0.1875
- w_state: bfloat16 [1024, 256], replicated, may hold values from -0.015625 to 0.015625
- w_out: bfloat16 [1024, 2048], P(None, 'heads'), may hold values from -0.125 to 0.125
Outputs:
- d_tokens: bfloat16 [4, 2048, 1024], P('seq', 'order', 'heads')
- d_w_inner: float32 [1024, 2048], P(('order', 'seq'), 'heads')
- d_w_state: float32 [1024, 256], P(('order', 'heads', 'seq'))
- d_w_out: float32 [1024, 2048], P(('order', 'seq'), 'heads')
The draws below stay inside these ranges and needn't reach their ends.
Inputs may be any that keep to these rules, and one draw needn't show every extreme that they name: `node_order`: within each aligned block of 512 positions of a sequence, the entries are a permutation of that block's positions. `decays`: decay factors of each position and head.
All inputs are finite; a program needn't handle non-finite values.
Results may differ from the reference program's by a relative error of at most 0.0057.
Values sent between devices are 32-bit elements; how exact they have to be, the bound alone decides.
No kernel may reach another device: no remote copies, remote signals or barrier semaphores. Data moves between devices by JAX's collectives and lax.ppermute only.
A program may use at most 128 MiB of HBM per device.

```python
import math
import jax
import jax.numpy as jnp
from jax import lax

D = 1024
H = 32
P_SIZE = 64
N = 128
Q = 256
TOK_DEV = 512
INNER = 2048
STRAND_SPAN = 2048
STRAND_TOTAL = 4


def draw_node_order(key, part):
    segments = STRAND_SPAN // TOK_DEV
    stochastic_seeds = jax.random.split(key, STRAND_TOTAL * segments)
    shuffled = jax.vmap(lambda one_key: jax.random.permutation(one_key, TOK_DEV))(stochastic_seeds)
    shuffled = shuffled.reshape(STRAND_TOTAL, segments, TOK_DEV) + (jnp.arange(segments) * TOK_DEV)[None, :, None]
    return shuffled.reshape(STRAND_TOTAL, STRAND_SPAN).astype(jnp.int32)


def draw_decays(key, part):
    stochastic_seeds = jax.random.split(key, 7)
    slow_share = 0.5
    slow_heads = jax.random.uniform(stochastic_seeds[0], (1, 1, H)) < slow_share
    slow_rate = jnp.exp(jax.random.uniform(stochastic_seeds[1], (1, 1, H), minval=math.log(0.05), maxval=math.log(0.5))) / STRAND_SPAN
    fast_rate = jax.random.uniform(stochastic_seeds[2], (1, 1, H), minval=1.0 / 50.0, maxval=1.0 / 30.0)
    default_speed = jnp.where(slow_heads, slow_rate, fast_rate)
    segments = STRAND_SPAN // TOK_DEV
    accelerator_scaling = jnp.exp(jax.random.uniform(stochastic_seeds[3], (STRAND_TOTAL, segments, 1, H), minval=math.log(0.5), maxval=math.log(2.0)))
    accelerator_scaling = jnp.broadcast_to(accelerator_scaling, (STRAND_TOTAL, segments, TOK_DEV, H)).reshape(STRAND_TOTAL, STRAND_SPAN, H)
    element_scaling = jax.random.uniform(stochastic_seeds[4], (STRAND_TOTAL, STRAND_SPAN, H), minval=0.5, maxval=1.5)
    spike_places = jax.random.randint(stochastic_seeds[5], (STRAND_TOTAL, 2), 0, STRAND_SPAN)
    spike_chosen = jnp.any(jnp.arange(STRAND_SPAN)[None, :, None] == spike_places[:, None, :], axis=2)
    spike_extent = jax.random.uniform(stochastic_seeds[6], (STRAND_TOTAL, STRAND_SPAN, 1), minval=0.5, maxval=0.8)
    natural_exponent = -default_speed * accelerator_scaling * element_scaling + jnp.where(spike_chosen[:, :, None], jnp.log(spike_extent), 0.0)
    return jnp.exp(natural_exponent).astype(jnp.float32)


def strengthened(values, key, source, target, blocks, factor):
    owner, partner = [(jnp.arange(values.shape[dim]) // (values.shape[dim] // blocks)).reshape([-1 if axis == dim else 1 for axis in range(values.ndim)]) for dim in (source, target)]
    chosen = jax.random.permutation(key, blocks)[partner]
    strong = (owner == chosen) | (owner == (partner + blocks // 2) % blocks)
    return jnp.where(strong, factor * values, values)


def block_levels(stream_key, dims, pieces, smallest, high):
    loudness = 1.0
    for position, shards_of in pieces:
        draws = jax.random.uniform(jax.random.fold_in(jax.random.fold_in(stream_key, 6), position), (shards_of,), jnp.float32, smallest / len(pieces), high / len(pieces))
        loudness = loudness * jnp.repeat(jnp.exp(draws), dims[position] // shards_of).reshape((-1,) + (1,) * (len(dims) - 1 - position))
    return loudness


def noise(own_key, dims, scale, most, shards=(), kind=jnp.bfloat16):
    values = scale * jax.random.normal(own_key, dims, jnp.float32)
    if shards:
        values = values * block_levels(own_key, dims, shards, -0.22, 0.18)
    return jnp.clip(values, -most, most).astype(kind)


def bell_draw_with(rng, extent, deviation, bound, pieces, heavy, dtype=jnp.bfloat16):
    result = deviation * jax.random.normal(rng, extent, jnp.float32)
    if pieces:
        result = result * block_levels(rng, extent, pieces, -0.22, 0.18)
    return jnp.clip(strengthened(result, jax.random.fold_in(rng, 3), *heavy), -bound, bound).astype(dtype)


def setup_inputs(seed: int = 0) -> dict:
    streams_of = jax.random.split(jax.random.key(seed), 8)
    return {
        "tokens": bell_draw_with(streams_of[0], (STRAND_TOTAL, STRAND_SPAN, D), 1.0, 6.0, ((0, 4), (1, 4)), (1, 2, 4, 2.0)),
        "cotangent": bell_draw_with(streams_of[1], (STRAND_TOTAL, STRAND_SPAN, D), 0.125, 1.0, ((0, 4), (1, 4)), (1, 2, 4, 2.0)),
        "node_order": draw_node_order(jax.random.fold_in(streams_of[7], 71), 0),
        "decays": draw_decays(jax.random.fold_in(streams_of[7], 71), 0),
        "w_inner": noise(streams_of[4], (D, INNER), D ** -0.5, 0.1875, ((1, 2),)),
        "w_state": noise(streams_of[5], (D, 2 * N), (D * N) ** -0.5, 0.015625),
        "w_out": noise(streams_of[6], (D, INNER), INNER ** -0.5, 0.125, ((1, 2),)),
    }


highest = lax.Precision.HIGHEST


def decay_table(log_rates):
    cumulative = jnp.cumsum(log_rates, axis=0).T
    length = log_rates.shape[0]
    causal = (jnp.arange(length)[:, None] >= jnp.arange(length)[None, :])[None]
    spread = cumulative[:, :, None] - cumulative[:, None, :]
    decay_mask = jnp.where(causal, jnp.exp(jnp.where(causal, spread, 0.0)), 0.0)
    return cumulative, decay_mask


def block_states(inner_x, b_mat, c_mat, inner_dy, log_rates):
    cumulative = jnp.cumsum(log_rates, axis=0).T
    last_sum = cumulative[:, -1]
    to_end = jnp.exp(last_sum[:, None] - cumulative).T
    from_start = jnp.exp(cumulative).T
    forward_part = jnp.einsum('shp,sn->hpn', inner_x * to_end[:, :, None], b_mat, precision=highest)
    backward_part = jnp.einsum('shp,sn->hpn', inner_dy * from_start[:, :, None], c_mat, precision=highest)
    return last_sum, forward_part, backward_part


def block_outputs(inner_x, b_mat, c_mat, inner_dy, log_rates, state_in, adjoint_in):
    cumulative, decay_mask = decay_table(log_rates)
    last_sum = cumulative[:, -1:]
    grow_in = jnp.exp(cumulative).T[:, :, None]
    decay_out = jnp.exp(last_sum - cumulative).T[:, :, None]
    scores = jnp.dot(c_mat, b_mat.T, precision=highest)
    weights = decay_mask * scores[None]
    out_y = jnp.einsum('hts,shp->thp', weights, inner_x, precision=highest)
    out_y = out_y + jnp.einsum('hpn,tn->thp', state_in, c_mat, precision=highest) * grow_in
    out_dx = jnp.einsum('hst,shp->thp', weights, inner_dy, precision=highest)
    out_dx = out_dx + jnp.einsum('hpn,tn->thp', adjoint_in, b_mat, precision=highest) * decay_out
    pair_dots = jnp.einsum('thp,shp->hts', inner_dy, inner_x, precision=highest)
    masked = decay_mask * pair_dots
    out_dc = jnp.einsum('hts,sn->tn', masked, b_mat, precision=highest)
    out_dc = out_dc + jnp.einsum('hpn,thp->tn', state_in, inner_dy * grow_in, precision=highest)
    out_db = jnp.einsum('hst,sn->tn', masked, c_mat, precision=highest)
    out_db = out_db + jnp.einsum('hpn,thp->tn', adjoint_in, inner_x * decay_out, precision=highest)
    return out_y, out_dx, out_db, out_dc


def advance(running, element):
    return jnp.exp(element[0])[:, None, None] * running + element[1], running


def sequence_terms(inner_x, b_mat, c_mat, inner_dy, log_rates):
    block_count = STRAND_SPAN // Q
    blocks = (inner_x.reshape(block_count, Q, H, P_SIZE), b_mat.reshape(block_count, Q, N),
              c_mat.reshape(block_count, Q, N), inner_dy.reshape(block_count, Q, H, P_SIZE),
              log_rates.reshape(block_count, Q, H))
    block_sums, forward_parts, backward_parts = lax.map(lambda element: block_states(*element), blocks)
    empty_state = jnp.zeros((H, P_SIZE, N), jnp.float32)
    final_fwd, starts = lax.scan(advance, empty_state, (block_sums, forward_parts))
    final_back, afters = lax.scan(advance, empty_state, (block_sums, backward_parts), reverse=True)
    results = lax.map(lambda element: block_outputs(*element), blocks + (starts, afters))
    return tuple(result_part.reshape(STRAND_SPAN, -1) for result_part in results)


def reference(tokens, cotangent, node_order, decays, w_inner, w_state, w_out):
    ordered = jnp.take_along_axis(tokens, node_order[:, :, None], axis=1)
    ordered_grad = jnp.take_along_axis(cotangent, node_order[:, :, None], axis=1)
    flat_in = ordered.reshape(STRAND_TOTAL * STRAND_SPAN, D)
    flat_grad = ordered_grad.reshape(STRAND_TOTAL * STRAND_SPAN, D)
    inner_x = jnp.dot(flat_in, w_inner, preferred_element_type=jnp.float32).astype(jnp.bfloat16)
    proj_bc = jnp.dot(flat_in, w_state, preferred_element_type=jnp.float32).astype(jnp.bfloat16)
    inner_dy = jnp.dot(flat_grad, w_out, preferred_element_type=jnp.float32).astype(jnp.bfloat16)
    log_rates = jnp.log(decays)

    def one_sequence(element):
        return sequence_terms(element[0].reshape(STRAND_SPAN, H, P_SIZE).astype(jnp.float32),
                              element[1][:, :N].astype(jnp.float32),
                              element[1][:, N:].astype(jnp.float32),
                              element[2].reshape(STRAND_SPAN, H, P_SIZE).astype(jnp.float32),
                              element[3])

    seq_y, seq_dx, seq_db, seq_dc = lax.map(one_sequence, (inner_x.reshape(STRAND_TOTAL, STRAND_SPAN, INNER),
                                                           proj_bc.reshape(STRAND_TOTAL, STRAND_SPAN, 2 * N),
                                                           inner_dy.reshape(STRAND_TOTAL, STRAND_SPAN, INNER),
                                                           log_rates))
    out_y = seq_y.reshape(STRAND_TOTAL * STRAND_SPAN, INNER).astype(jnp.bfloat16)
    grad_x = seq_dx.reshape(STRAND_TOTAL * STRAND_SPAN, INNER).astype(jnp.bfloat16)
    grad_bc = jnp.concatenate([seq_db, seq_dc], axis=-1).reshape(STRAND_TOTAL * STRAND_SPAN, 2 * N)
    contract_rows = (((0,), (0,)), ((), ()))
    d_w_inner = lax.dot_general(flat_in, grad_x, contract_rows, preferred_element_type=jnp.float32)
    d_w_out = lax.dot_general(flat_grad, out_y, contract_rows, preferred_element_type=jnp.float32)
    d_w_state = lax.dot_general(flat_in.astype(jnp.float32), grad_bc, contract_rows, precision=highest)
    back_in = jnp.dot(grad_x, w_inner.T, preferred_element_type=jnp.float32)
    back_in = back_in + jnp.dot(grad_bc, w_state.astype(jnp.float32).T, precision=highest)
    ordered_back = back_in.astype(jnp.bfloat16).reshape(STRAND_TOTAL, STRAND_SPAN, D)
    d_tokens = jax.vmap(lambda target_rows, values: jnp.zeros_like(values).at[target_rows].set(values))(node_order, ordered_back)
    return d_tokens, d_w_inner, d_w_state, d_w_out
```

```python
import functools

import jax
import jax.numpy as jnp
from jax import lax
from jax.experimental import pallas as pl
from jax.experimental.pallas import tpu as pltpu
from jax.sharding import PartitionSpec as P

CHUNK = 128
GROUPS = 4
LIMIT = 48 * 1024 * 1024
f32 = jnp.float32
bf16 = jnp.bfloat16


def dot(a, b, ca=1, cb=0):
    return lax.dot_general(a, b, (((ca,), (cb,)), ((), ())), preferred_element_type=f32)


def log2(n):
    bits = n.bit_length() - 1
    assert 1 << bits == n
    return bits


def place(index, order):
    out = 0
    for rank, bit in enumerate(order):
        out = out + (((index >> bit) & 1) << (len(order) - 1 - rank))
    return out


def block_at(position, order):
    out = 0
    for rank, bit in enumerate(order):
        out |= ((position >> (len(order) - 1 - rank)) & 1) << bit
    return out


def spread(values, first, heads, size):
    total = values.shape[1]
    row = lax.broadcasted_iota(jnp.int32, (total, heads * size), 0)
    col = lax.broadcasted_iota(jnp.int32, (total, heads * size), 1)
    low = (row - first) * size
    pick = jnp.where((col >= low) & (col < low + size), 1.0, 0.0).astype(bf16)
    high = values.astype(bf16)
    rest = values - high.astype(f32)
    middle = rest.astype(bf16)
    last = (rest - middle.astype(f32)).astype(bf16)
    return dot(high, pick) + dot(middle, pick) + dot(last, pick)


def triangle(upper):
    row = lax.broadcasted_iota(jnp.int32, (CHUNK, CHUNK), 0)
    col = lax.broadcasted_iota(jnp.int32, (CHUNK, CHUNK), 1)
    return row <= col if upper else row >= col


def one_hot_rows(offsets, rows):
    node = lax.broadcasted_iota(jnp.int32, (rows, offsets.shape[1]), 0)
    return jnp.where(node == offsets, 1.0, 0.0).astype(bf16)


def order_kernel(x_order, y_order, ids, off, tokens, cot, decays, w_state,
                 ordered, ordered_grad, ordered_t, grad_t, sc, sb, cum):
    me, base = ids[0], ids[1]
    rows, width = tokens.shape
    blocks = 1 << len(x_order)
    size = width // blocks
    hot = one_hot_rows(off[...] - base, rows)
    half = width // 2
    for source, plain, turned, order in ((tokens, ordered, ordered_t, x_order), (cot, ordered_grad, grad_t, y_order)):
        plain[...] = dot(hot, source[...], 0, 0).astype(bf16)
        for part in range(2):
            value = dot(source[:, part * half:(part + 1) * half], hot, 0, 0).astype(bf16)
            for block in range(blocks // 2):
                where = place((block + part * (blocks // 2)) ^ me, order)
                turned[pl.ds(pl.multiple_of(where * size, size), size), :] = value[block * size:(block + 1) * size]
    bc = dot(ordered[...], w_state[...]).astype(bf16)
    state = bc.shape[1] // 2
    lower = triangle(False)
    upper = triangle(True)
    ones = jnp.where(lower, 1.0, 0.0)
    rates = jnp.log(decays[...])
    for k in range(rows // CHUNK):
        span = slice(k * CHUNK, (k + 1) * CHUNK)
        b, c = bc[span, :state], bc[span, state:]
        sc[span, :CHUNK] = jnp.where(lower, dot(c, b, 1, 1), 0.0).astype(bf16)
        sc[span, CHUNK:] = c
        sb[span, :CHUNK] = jnp.where(upper, dot(b, c, 1, 1), 0.0).astype(bf16)
        sb[span, CHUNK:] = b
        cum[span, :] = jnp.dot(ones, rates[span], precision=lax.Precision.HIGHEST, preferred_element_type=f32)


def chunk_rows(cum_x, k):
    part = cum_x[k * CHUNK:(k + 1) * CHUNK]
    return part, part[CHUNK // 2 - 1:CHUNK // 2], part[CHUNK - 1:CHUNK]


def states_kernel(first, heads, size, ordered, ordered_grad, w_inner, w_out, sc, sb, cum,
                  xs, ys, fwd, bwd, total):
    cum_x = spread(cum[...], first, heads, size)
    x = dot(ordered[...], w_inner[...]).astype(bf16).astype(f32)
    dy = dot(ordered_grad[...], w_out[...]).astype(bf16).astype(f32)
    count = cum_x.shape[0] // CHUNK
    forward, back, decay = [], [], []
    for k in range(count):
        span = slice(k * CHUNK, (k + 1) * CHUNK)
        part, mid, last = chunk_rows(cum_x, k)
        x_s = (x[span] * jnp.exp(mid - part)).astype(bf16)
        y_s = (dy[span] * jnp.exp(part - mid)).astype(bf16)
        xs[span, :] = x_s
        ys[span, :] = y_s
        forward.append(jnp.exp(last - mid) * dot(sb[span, CHUNK:], x_s, 0, 0))
        back.append(jnp.exp(mid) * dot(sc[span, CHUNK:], y_s, 0, 0))
        decay.append(jnp.exp(last))
    run, run_back, factor = forward[0], back[-1], decay[0]
    for k in range(1, count):
        run = decay[k] * run + forward[k]
        factor = factor * decay[k]
        run_back = decay[count - 1 - k] * run_back + back[count - 1 - k]
    fwd[...] = run
    bwd[...] = run_back
    total[...] = factor


def outputs_kernel(first, heads, size, xs, ys, sc, sb, cum, fwd_in, bwd_in, ordered_t, grad_t,
                   keep_in, send_in, keep_out, send_out, grad_x, grad_bc, y_all):
    cum_x = spread(cum[...], first, heads, size)
    count = cum_x.shape[0] // CHUNK
    lower = triangle(False)
    upper = triangle(True)
    starts, afters = [fwd_in[...]], [bwd_in[...]]
    for k in range(count - 1):
        span = slice(k * CHUNK, (k + 1) * CHUNK)
        _, mid, last = chunk_rows(cum_x, k)
        starts.append(jnp.exp(last) * starts[-1] + jnp.exp(last - mid) * dot(sb[span, CHUNK:], xs[span, :], 0, 0))
    for k in range(count - 1, 0, -1):
        span = slice(k * CHUNK, (k + 1) * CHUNK)
        _, mid, last = chunk_rows(cum_x, k)
        afters.insert(0, jnp.exp(last) * afters[0] + jnp.exp(mid) * dot(sc[span, CHUNK:], ys[span, :], 0, 0))
    for k in range(count):
        span = slice(k * CHUNK, (k + 1) * CHUNK)
        part, mid, last = chunk_rows(cum_x, k)
        x_s, y_s = xs[span, :], ys[span, :]
        x_rows = jnp.concatenate([x_s, (starts[k] * jnp.exp(mid)).astype(bf16)], axis=0)
        y_rows = jnp.concatenate([y_s, (afters[k] * jnp.exp(last - mid)).astype(bf16)], axis=0)
        y_all[span, :] = (jnp.exp(part - mid) * dot(sc[span, :], x_rows)).astype(bf16)
        grad_x[span, :] = (jnp.exp(mid - part) * dot(sb[span, :], y_rows)).astype(bf16)
        by_y = dot(y_s, x_rows, 1, 1)
        by_x = dot(x_s, y_rows, 1, 1)
        pairs = jnp.where(lower, by_y[:, :CHUNK], 0.0).astype(bf16)
        turned = jnp.where(upper, by_x[:, :CHUNK], 0.0).astype(bf16)
        state = by_x.shape[1] - CHUNK
        grad_bc[span, :state] = dot(turned, sc[span, CHUNK:]) + by_x[:, CHUNK:]
        grad_bc[span, state:] = dot(pairs, sb[span, CHUNK:]) + by_y[:, CHUNK:]
    half = ordered_t.shape[0] // 2
    send_in[...] = dot(ordered_t[half:, :], grad_x[...])
    send_out[...] = dot(grad_t[half:, :], y_all[...])
    keep_in[...] = dot(ordered_t[:half, :], grad_x[...])
    keep_out[...] = dot(grad_t[:half, :], y_all[...])


def back_kernel(groups, x_order, s_order, ids, *refs):
    grads, sums = refs[:groups], refs[groups:2 * groups]
    w_inner, w_state, ordered_t, keep, send, state_keep, state_send, table = refs[2 * groups:]
    me, side, me_state = ids[0], ids[2], ids[3]
    grad_bc = sums[0][...]
    for part in sums[1:]:
        grad_bc = grad_bc + part[...]
    grad_bc = grad_bc.astype(bf16)
    half = w_inner.shape[0] // 2
    for out, which in ((send, 1 - side), (keep, side)):
        rows = pl.ds(pl.multiple_of(which * half, half), half)
        value = dot(grad_bc, w_state[rows, :], 1, 1)
        start = 0
        for part in grads:
            cols = part.shape[1]
            value = value + dot(part[...], w_inner[rows, start:start + cols], 1, 1)
            start += cols
        out[...] = value
    blocks = 1 << len(x_order)
    size = ordered_t.shape[0] // blocks
    fine = ordered_t.shape[0] >> len(s_order)
    step = ordered_t.shape[0] // 4
    for quarter in range(4):
        value = dot(ordered_t[quarter * step:(quarter + 1) * step, :], grad_bc)
        for piece in range(step // fine):
            row = quarter * step + piece * fine
            block = block_at(row // size, x_order) ^ me
            index = block * (size // fine) + (row % size) // fine
            where = place(index ^ me_state, s_order)
            table[pl.ds(pl.multiple_of(where * fine, fine), fine), :] = value[piece * fine:(piece + 1) * fine]
    middle = ordered_t.shape[0] // 2
    state_keep[...] = table[:middle, :]
    state_send[...] = table[middle:, :]


def place_kernel(ids, off, keep, came, out):
    hot = one_hot_rows(off[...] - ids[1], out.shape[0])
    out[...] = dot(hot, (keep[...] + came[...]).astype(bf16)).astype(bf16)


def flips(axis, bit):
    return [(i, i ^ (1 << bit)) for i in range(lax.axis_size(axis))]


def halving(keep, send, hops):
    parts = [keep]
    for rank, (axis, bit) in enumerate(hops):
        parts.append(lax.ppermute(send, axis, flips(axis, bit)))
        rows = send.shape[0]
        if rank + 1 < len(hops):
            rows //= 2
            send = sum(part[rows:2 * rows] for part in parts[1:]) + parts[0][rows:2 * rows]
            parts = [part[:rows] for part in parts]
    out = parts[0]
    for part in parts[1:]:
        out = out + part
    return out


def carries(forward, back, total):
    count, mine = lax.axis_size("order"), lax.axis_index("order")
    run, run_back = jnp.zeros_like(forward), jnp.zeros_like(back)
    for k in range(1, count):
        up, down = total * run + forward, total * run_back + back
        if count % 2 == 0:
            message = jnp.where(mine == k - 1, up, down)
            came = came_back = lax.ppermute(message, "order", [(k - 1, k), (count - k, count - k - 1)])
        else:
            came = lax.ppermute(up, "order", [(k - 1, k)])
            came_back = lax.ppermute(down, "order", [(count - k, count - k - 1)])
        run = jnp.where(mine == k, came, run)
        run_back = jnp.where(mine == count - k - 1, came_back, run_back)
    return run, run_back


def whole(array):
    return pl.BlockSpec(array.shape, lambda *_: (0,) * len(array.shape))


def call(kernel, outs, args, name, scratch=(), specs=None, flops=0):
    specs = specs or {}
    in_specs = []
    for i, arg in enumerate(args):
        if i in specs:
            in_specs.append(specs[i])
        elif arg.dtype == jnp.int32 and arg.ndim == 1:
            in_specs.append(pl.BlockSpec(memory_space=pltpu.SMEM))
        else:
            in_specs.append(whole(arg))
    moved = sum(a.size * a.dtype.itemsize for a in list(args) + list(outs))
    return pl.pallas_call(
        kernel,
        out_shape=tuple(outs),
        grid=(1,),
        in_specs=in_specs,
        out_specs=tuple(whole(o) for o in outs),
        scratch_shapes=list(scratch),
        compiler_params=pltpu.CompilerParams(vmem_limit_bytes=LIMIT),
        cost_estimate=pl.CostEstimate(flops=int(flops), bytes_accessed=int(moved), transcendentals=0),
        name=name,
    )(*args)


def per_device(tokens, cotangent, node_order, decays, w_inner, w_state, w_out):
    assert tokens.shape[0] == 1
    tokens, cotangent, decays = tokens[0], cotangent[0], decays[0]
    rows, width = tokens.shape
    heads = decays.shape[1]
    inner = w_inner.shape[1]
    size = inner // heads
    state = w_state.shape[1] // 2
    cols = inner // GROUPS
    group_heads = heads // GROUPS
    n_order, n_heads, n_seq = (lax.axis_size(a) for a in ("order", "heads", "seq"))
    o, h, s = (lax.axis_index(a) for a in ("order", "heads", "seq"))
    seq_bits, head_bits, order_bits = log2(n_seq), log2(n_heads), log2(n_order)
    seq_hops = [("seq", b) for b in range(seq_bits)]
    order_hops = [("order", b) for b in range(order_bits)]
    x_hops = seq_hops + order_hops
    y_hops = seq_hops[::-1] + order_hops
    s_hops = [("heads", b) for b in range(head_bits)] + order_hops + seq_hops
    shift = {"seq": 0, "order": seq_bits}
    shift_state = {"seq": 0, "heads": seq_bits, "order": seq_bits + head_bits}
    x_order = [shift[a] + b for a, b in x_hops]
    y_order = [shift[a] + b for a, b in y_hops]
    s_order = [shift_state[a] + b for a, b in s_hops]
    ids = jnp.stack([o * n_seq + s, o * rows, h, (o * n_heads + h) * n_seq + s]).astype(jnp.int32)
    S = jax.ShapeDtypeStruct
    full = S((rows, width), bf16)
    turned = S((width, rows), bf16)
    wide = S((rows, CHUNK + state), bf16)
    ordered, ordered_grad, ordered_t, grad_t, sc, sb, cum = call(
        functools.partial(order_kernel, x_order, y_order),
        [full, full, turned, turned, wide, wide, S((rows, heads), f32)],
        [ids, node_order, tokens, cotangent, decays, w_state], "order",
        flops=10 * rows * rows * width)
    states = []
    for g in range(GROUPS):
        column = pl.BlockSpec((width, cols), functools.partial(lambda g, _: (0, g), g))
        states.append(call(
            functools.partial(states_kernel, g * group_heads, group_heads, size),
            [S((rows, cols), bf16)] * 2 + [S((state, cols), f32)] * 2 + [S((1, cols), f32)],
            [ordered, ordered_grad, w_inner, w_out, sc, sb, cum], f"states_{g}", specs={2: column, 3: column},
            flops=4 * rows * width * cols))
    in_parts, out_parts, grads, sums = [], [], [], []
    for g in range(GROUPS):
        xs, ys, fwd, bwd, total = states[g]
        run, run_back = carries(fwd, bwd, total)
        half = S((width // 2, cols), f32)
        keep_in, send_in, keep_out, send_out, grad_x, grad_bc = call(
            functools.partial(outputs_kernel, g * group_heads, group_heads, size),
            [half] * 4 + [S((rows, cols), bf16), S((rows, 2 * state), f32)],
            [xs, ys, sc, sb, cum, run, run_back, ordered_t, grad_t], f"outputs_{g}",
            scratch=[pltpu.VMEM((rows, cols), bf16)],
            flops=4 * rows * width * cols)
        in_parts.append(halving(keep_in, send_in, x_hops))
        out_parts.append(halving(keep_out, send_out, y_hops))
        grads.append(grad_x)
        sums.append(grad_bc)
    piece = S((rows, width // 2), f32)
    half_state = S((width // 2, 2 * state), f32)
    keep, send, state_keep, state_send = call(
        functools.partial(back_kernel, GROUPS, x_order, s_order),
        [piece, piece, half_state, half_state],
        [ids] + grads + sums + [w_inner, w_state, ordered_t], "back",
        scratch=[pltpu.VMEM((width, 2 * state), f32)],
        flops=2 * rows * width * inner)
    came = lax.ppermute(send, "heads", flips("heads", 0))
    d_tokens = call(place_kernel, [S((rows, width // 2), bf16)], [ids, node_order, keep, came], "place",
                    flops=rows * rows * width)[0]
    d_w_state = halving(state_keep, state_send, s_hops)
    d_w_inner = jnp.concatenate(in_parts, axis=1)
    d_w_out = jnp.concatenate(out_parts, axis=1)
    return d_tokens[None], d_w_inner, d_w_state, d_w_out


def solution(mesh):
    in_specs = (
        P("seq", "order", None),
        P("seq", "order", None),
        P("seq", "order"),
        P("seq", "order", "heads"),
        P(None, "heads"),
        P(),
        P(None, "heads"),
    )
    out_specs = (
        P("seq", "order", "heads"),
        P(("order", "seq"), "heads"),
        P(("order", "heads", "seq"), None),
        P(("order", "seq"), "heads"),
    )
    return jax.shard_map(
        per_device, mesh=mesh, in_specs=in_specs, out_specs=out_specs, check_vma=False
    )
```

```python
import functools

import jax
import jax.numpy as jnp
from jax import lax
from jax.experimental import pallas as pl
from jax.experimental.pallas import tpu as pltpu
from jax.sharding import PartitionSpec as P

CHUNK = 128
ROUNDS = 2
LIMIT = 48 * 1024 * 1024
f32 = jnp.float32
bf16 = jnp.bfloat16


def dot(a, b, ca=1, cb=0):
    return lax.dot_general(a, b, (((ca,), (cb,)), ((), ())), preferred_element_type=f32)


def log2(n):
    bits = n.bit_length() - 1
    assert 1 << bits == n
    return bits


def place(index, order):
    out = 0
    for rank, bit in enumerate(order):
        out = out + (((index >> bit) & 1) << (len(order) - 1 - rank))
    return out


def spread(values, first, heads, size):
    total = values.shape[1]
    row = lax.broadcasted_iota(jnp.int32, (total, heads * size), 0)
    col = lax.broadcasted_iota(jnp.int32, (total, heads * size), 1)
    low = (row - first) * size
    pick = jnp.where((col >= low) & (col < low + size), 1.0, 0.0).astype(bf16)
    high = values.astype(bf16)
    rest = values - high.astype(f32)
    middle = rest.astype(bf16)
    last = (rest - middle.astype(f32)).astype(bf16)
    return dot(high, pick) + dot(middle, pick) + dot(last, pick)


def triangle(upper):
    row = lax.broadcasted_iota(jnp.int32, (CHUNK, CHUNK), 0)
    col = lax.broadcasted_iota(jnp.int32, (CHUNK, CHUNK), 1)
    return row <= col if upper else row >= col


def one_hot_rows(offsets, rows):
    node = lax.broadcasted_iota(jnp.int32, (rows, offsets.shape[1]), 0)
    return jnp.where(node == offsets, 1.0, 0.0).astype(bf16)


def chunk_rows(cum_x, k):
    part = cum_x[k * CHUNK:(k + 1) * CHUNK]
    return part, part[CHUNK // 2 - 1:CHUNK // 2], part[CHUNK - 1:CHUNK]


def end_states(cum_x, x, dy, sc, sb, xs, ys, fwd, bwd, total):
    count = cum_x.shape[0] // CHUNK
    forward, back, decay = [], [], []
    for k in range(count):
        span = slice(k * CHUNK, (k + 1) * CHUNK)
        part, mid, last = chunk_rows(cum_x, k)
        x_s = (x[span] * jnp.exp(mid - part)).astype(bf16)
        y_s = (dy[span] * jnp.exp(part - mid)).astype(bf16)
        xs[span, :] = x_s
        ys[span, :] = y_s
        forward.append(jnp.exp(last - mid) * dot(sb[span, CHUNK:], x_s, 0, 0))
        back.append(jnp.exp(mid) * dot(sc[span, CHUNK:], y_s, 0, 0))
        decay.append(jnp.exp(last))
    run, run_back, factor = forward[0], back[-1], decay[0]
    for k in range(1, count):
        run = decay[k] * run + forward[k]
        factor = factor * decay[k]
        run_back = decay[count - 1 - k] * run_back + back[count - 1 - k]
    fwd[...] = run
    bwd[...] = run_back
    total[...] = factor


def order_kernel(heads, size, ids, off, tokens, cot, decays, w_state, w_inner, w_out,
                 ordered, ordered_grad, early_a, early_b, sc, sb, cum, xs, ys, fwd, bwd, total):
    base, side = ids[1], ids[2]
    rows, width = tokens.shape
    half = width // 2
    hot = one_hot_rows(off[...] - base, rows)
    ordered[...] = dot(hot, tokens[...], 0, 0).astype(bf16)
    ordered_grad[...] = dot(hot, cot[...], 0, 0).astype(bf16)
    first = jnp.where(side == 0, ordered[:, :half].astype(f32), ordered[:, half:].astype(f32))
    second = jnp.where(side == 0, ordered_grad[:, :half].astype(f32), ordered_grad[:, half:].astype(f32))
    early_a[...] = jnp.where(ids[4] == 0, second, first)
    early_b[...] = jnp.where(ids[5] == 0, second, first)
    bc = dot(ordered[...], w_state[...]).astype(bf16)
    state = bc.shape[1] // 2
    lower = triangle(False)
    upper = triangle(True)
    ones = jnp.where(lower, 1.0, 0.0)
    rates = jnp.log(decays[...])
    for k in range(rows // CHUNK):
        span = slice(k * CHUNK, (k + 1) * CHUNK)
        b, c = bc[span, :state], bc[span, state:]
        sc[span, :CHUNK] = jnp.where(lower, dot(c, b, 1, 1), 0.0).astype(bf16)
        sc[span, CHUNK:] = c
        sb[span, :CHUNK] = jnp.where(upper, dot(b, c, 1, 1), 0.0).astype(bf16)
        sb[span, CHUNK:] = b
        cum[span, :] = jnp.dot(ones, rates[span], precision=lax.Precision.HIGHEST, preferred_element_type=f32)
    cum_x = spread(cum[...], 0, heads, size)
    x = dot(ordered[...], w_inner[...]).astype(bf16).astype(f32)
    dy = dot(ordered_grad[...], w_out[...]).astype(bf16).astype(f32)
    end_states(cum_x, x, dy, sc, sb, xs, ys, fwd, bwd, total)


def states_kernel(first, heads, size, ordered, ordered_grad, w_inner, w_out, sc, sb, cum,
                  xs, ys, fwd, bwd, total):
    cum_x = spread(cum[...], first, heads, size)
    x = dot(ordered[...], w_inner[...]).astype(bf16).astype(f32)
    dy = dot(ordered_grad[...], w_out[...]).astype(bf16).astype(f32)
    end_states(cum_x, x, dy, sc, sb, xs, ys, fwd, bwd, total)


def turn_kernel(a_order, b_order, ids, ordered, ordered_grad, near_a, far_a, near_b, far_b, left_a, left_b):
    me, side = ids[0], ids[2]
    rows, width = ordered.shape
    half = width // 2
    blocks = 1 << len(a_order)
    size = width // blocks
    for left, order, role, near, far in ((left_a, a_order, ids[4], near_a, far_a), (left_b, b_order, ids[5], near_b, far_b)):
        for part in range(2):
            span = slice(part * half, (part + 1) * half)
            own = jnp.where(role == 0, ordered[:, span].astype(f32), ordered_grad[:, span].astype(f32)).astype(bf16)
            other = jnp.where(side == part, near[...], far[...]).astype(bf16)
            value = jnp.concatenate([own.T, other.T], axis=1)
            for block in range(blocks // 2):
                where = place((block + part * (blocks // 2)) ^ me, order)
                left[pl.ds(pl.multiple_of(where * size, size), size), :] = value[block * size:(block + 1) * size]


def outputs_kernel(first, heads, size, ids, xs, ys, sc, sb, cum, fwd_in, bwd_in,
                   own_a, send_a, own_b, send_b, grad_x, grad_bc):
    cum_x = spread(cum[...], first, heads, size)
    count = cum_x.shape[0] // CHUNK
    lower = triangle(False)
    upper = triangle(True)
    starts, afters = [fwd_in[...]], [bwd_in[...]]
    for k in range(count - 1):
        span = slice(k * CHUNK, (k + 1) * CHUNK)
        _, mid, last = chunk_rows(cum_x, k)
        starts.append(jnp.exp(last) * starts[-1] + jnp.exp(last - mid) * dot(sb[span, CHUNK:], xs[span, :], 0, 0))
    for k in range(count - 1, 0, -1):
        span = slice(k * CHUNK, (k + 1) * CHUNK)
        _, mid, last = chunk_rows(cum_x, k)
        afters.insert(0, jnp.exp(last) * afters[0] + jnp.exp(mid) * dot(sc[span, CHUNK:], ys[span, :], 0, 0))
    cols = xs.shape[1] // 2
    for k in range(count):
        span = slice(k * CHUNK, (k + 1) * CHUNK)
        part, mid, last = chunk_rows(cum_x, k)
        x_s, y_s = xs[span, :], ys[span, :]
        x_rows = jnp.concatenate([x_s, (starts[k] * jnp.exp(mid)).astype(bf16)], axis=0)
        y_rows = jnp.concatenate([y_s, (afters[k] * jnp.exp(last - mid)).astype(bf16)], axis=0)
        y = (jnp.exp(part - mid) * dot(sc[span, :], x_rows)).astype(bf16)
        dx = (jnp.exp(mid - part) * dot(sb[span, :], y_rows)).astype(bf16)
        grad_x[span, :] = dx
        y, dx = y.astype(f32), dx.astype(f32)
        for own, send, role, cut in ((own_a, send_a, ids[4], slice(0, cols)), (own_b, send_b, ids[5], slice(cols, 2 * cols))):
            own[span, :] = jnp.where(role == 0, dx[:, cut], y[:, cut]).astype(bf16)
            send[span, :] = jnp.where(role == 0, y[:, cut], dx[:, cut])
        by_y = dot(y_s, x_rows, 1, 1)
        by_x = dot(x_s, y_rows, 1, 1)
        pairs = jnp.where(lower, by_y[:, :CHUNK], 0.0).astype(bf16)
        turned = jnp.where(upper, by_x[:, :CHUNK], 0.0).astype(bf16)
        state = by_x.shape[1] - CHUNK
        grad_bc[span, :state] = dot(turned, sc[span, CHUNK:]) + by_x[:, CHUNK:]
        grad_bc[span, state:] = dot(pairs, sb[span, CHUNK:]) + by_y[:, CHUNK:]


def grads_kernel(left_a, left_b, own_a, came_a, own_b, came_b, keep_a, send_a, keep_b, send_b):
    half = left_a.shape[0] // 2
    for left, own, came, keep, send in ((left_a, own_a, came_a, keep_a, send_a), (left_b, own_b, came_b, keep_b, send_b)):
        right = jnp.concatenate([own[...], came[...].astype(bf16)], axis=0)
        send[...] = dot(left[half:, :], right)
        keep[...] = dot(left[:half, :], right)


def back_kernel(rounds, s_order, ids, *refs):
    grads, sums = refs[:rounds], refs[rounds:2 * rounds]
    w_inner, w_state, ordered, keep, send, state_keep, state_send, table = refs[2 * rounds:]
    side, me_state = ids[2], ids[3]
    grad_bc = sums[0][...]
    for part in sums[1:]:
        grad_bc = grad_bc + part[...]
    grad_bc = grad_bc.astype(bf16)
    width = ordered.shape[1]
    half = width // 2
    for out, which in ((send, 1 - side), (keep, side)):
        rows = pl.ds(pl.multiple_of(which * half, half), half)
        value = dot(grad_bc, w_state[rows, :], 1, 1)
        start = 0
        for part in grads:
            cols = part.shape[1]
            value = value + dot(part[...], w_inner[rows, start:start + cols], 1, 1)
            start += cols
        out[...] = value
    fine = width >> len(s_order)
    step = width // 4
    for quarter in range(4):
        value = dot(ordered[:, quarter * step:(quarter + 1) * step], grad_bc, 0, 0)
        for piece in range(step // fine):
            index = (quarter * step) // fine + piece
            where = place(index ^ me_state, s_order)
            table[pl.ds(pl.multiple_of(where * fine, fine), fine), :] = value[piece * fine:(piece + 1) * fine]
    state_keep[...] = table[:half, :]
    state_send[...] = table[half:, :]


def place_kernel(ids, off, keep, came, out):
    hot = one_hot_rows(off[...] - ids[1], out.shape[0])
    out[...] = dot(hot, (keep[...] + came[...]).astype(bf16)).astype(bf16)


def flips(axis, bit):
    return [(i, i ^ (1 << bit)) for i in range(lax.axis_size(axis))]


def total_of(parts, start, stop):
    out = parts[0][..., start:stop, :]
    for part in parts[1:]:
        out = out + part[..., start:stop, :]
    return out


def halving(parts, hops):
    rows = parts[0].shape[-2]
    for axis, bit in hops:
        rows //= 2
        parts = [p[..., :2 * rows, :] for p in parts]
        came = lax.ppermute(total_of(parts, rows, 2 * rows), axis, flips(axis, bit))
        parts = [p[..., :rows, :] for p in parts] + [came]
    return total_of(parts, 0, rows)


def carries(forward, back, total):
    count, mine = lax.axis_size("order"), lax.axis_index("order")
    run, run_back = jnp.zeros_like(forward), jnp.zeros_like(back)
    first = None
    for k in range(1, count):
        up, down = total * run + forward, total * run_back + back
        if count % 2 == 0:
            message = jnp.where(mine == k - 1, up, down)
            came = came_back = lax.ppermute(message, "order", [(k - 1, k), (count - k, count - k - 1)])
        else:
            message = up
            came = lax.ppermute(up, "order", [(k - 1, k)])
            came_back = lax.ppermute(down, "order", [(count - k, count - k - 1)])
        first = message if first is None else first
        run = jnp.where(mine == k, came, run)
        run_back = jnp.where(mine == count - k - 1, came_back, run_back)
    return run, run_back, first


def whole(array):
    return pl.BlockSpec(array.shape, lambda *_: (0,) * len(array.shape))


def call(kernel, outs, args, name, scratch=(), specs=None, flops=0):
    specs = specs or {}
    in_specs = []
    for i, arg in enumerate(args):
        if i in specs:
            in_specs.append(specs[i])
        elif arg.dtype == jnp.int32 and arg.ndim == 1:
            in_specs.append(pl.BlockSpec(memory_space=pltpu.SMEM))
        else:
            in_specs.append(whole(arg))
    moved = sum(a.size * a.dtype.itemsize for a in list(args) + list(outs))
    return pl.pallas_call(
        kernel,
        out_shape=tuple(outs),
        grid=(1,),
        in_specs=in_specs,
        out_specs=tuple(whole(o) for o in outs),
        scratch_shapes=list(scratch),
        compiler_params=pltpu.CompilerParams(vmem_limit_bytes=LIMIT),
        cost_estimate=pl.CostEstimate(flops=int(flops), bytes_accessed=int(moved), transcendentals=0),
        name=name,
    )(*args)


def per_device(tokens, cotangent, node_order, decays, w_inner, w_state, w_out):
    assert tokens.shape[0] == 1
    tokens, cotangent, decays = tokens[0], cotangent[0], decays[0]
    rows, width = tokens.shape
    heads = decays.shape[1]
    inner = w_inner.shape[1]
    size = inner // heads
    state = w_state.shape[1] // 2
    cols = inner // ROUNDS
    round_heads = heads // ROUNDS
    n_order, n_heads, n_seq = (lax.axis_size(a) for a in ("order", "heads", "seq"))
    o, h, s = (lax.axis_index(a) for a in ("order", "heads", "seq"))
    seq_bits, head_bits, order_bits = log2(n_seq), log2(n_heads), log2(n_order)
    assert seq_bits == 2 and head_bits == 1
    order_hops = [("order", b) for b in range(order_bits)]
    a_hops = [("seq", 1)] + order_hops + [("seq", 0)]
    b_hops = [("seq", 0)] + order_hops + [("seq", 1)]
    s_hops = [("heads", 0)] + order_hops + [("seq", 0), ("seq", 1)]
    shift = {"seq": 0, "order": seq_bits}
    shift_state = {"seq": 0, "heads": seq_bits, "order": seq_bits + head_bits}
    a_order = [shift[a] + b for a, b in a_hops]
    b_order = [shift[a] + b for a, b in b_hops]
    s_order = [shift_state[a] + b for a, b in s_hops]
    role_a, role_b = s & 1, (s >> 1) & 1
    ids = jnp.stack([o * n_seq + s, o * rows, h, (o * n_heads + h) * n_seq + s, role_a, role_b]).astype(jnp.int32)
    S = jax.ShapeDtypeStruct
    full = S((rows, width), bf16)
    half_wide = S((rows, width // 2), f32)
    wide = S((rows, CHUNK + state), bf16)
    ends = [S((rows, cols), bf16)] * 2 + [S((state, cols), f32)] * 2 + [S((1, cols), f32)]

    def column(r):
        return pl.BlockSpec((width, cols), lambda _: (0, r))

    ordered, ordered_grad, early_a, early_b, sc, sb, cum, *first = call(
        functools.partial(order_kernel, round_heads, size),
        [full, full, half_wide, half_wide, wide, wide, S((rows, heads), f32)] + ends,
        [ids, node_order, tokens, cotangent, decays, w_state, w_inner, w_out], "order",
        specs={6: column(0), 7: column(0)}, flops=10 * rows * rows * width)
    rounds = [first]
    run, run_back, message = carries(*first[2:])
    incoming = [(run, run_back)]
    for r in range(1, ROUNDS):
        cum_r, _ = lax.optimization_barrier((cum, message))
        rounds.append(call(
            functools.partial(states_kernel, r * round_heads, round_heads, size), ends,
            [ordered, ordered_grad, w_inner, w_out, sc, sb, cum_r], f"states_{r}",
            specs={2: column(r), 3: column(r)}, flops=4 * rows * width * cols))
        run, run_back, message = carries(*rounds[r][2:])
        incoming.append((run, run_back))
    near_a = lax.ppermute(early_a, "seq", flips("seq", 0))
    near_b = lax.ppermute(early_b, "seq", flips("seq", 1))
    far_a = lax.ppermute(near_a, "heads", flips("heads", 0))
    far_b = lax.ppermute(near_b, "heads", flips("heads", 0))
    pair = S((width, 2 * rows), bf16)
    left_a, left_b = call(
        functools.partial(turn_kernel, a_order, b_order), [pair, pair],
        [ids, ordered, ordered_grad, near_a, far_a, near_b, far_b], "turn", flops=rows * width)
    part = cols // 2
    halves, grads, sums = [], [], []
    for r in range(ROUNDS):
        xs, ys = rounds[r][:2]
        own_a, send_a, own_b, send_b, grad_x, grad_bc = call(
            functools.partial(outputs_kernel, r * round_heads, round_heads, size),
            [S((rows, part), bf16), S((rows, part), f32)] * 2 + [S((rows, cols), bf16), S((rows, 2 * state), f32)],
            [ids, xs, ys, sc, sb, cum, *incoming[r]], f"outputs_{r}",
            flops=8 * rows * 256 * cols)
        grads.append(grad_x)
        sums.append(grad_bc)
        came_a = lax.ppermute(send_a, "seq", flips("seq", 0))
        came_b = lax.ppermute(send_b, "seq", flips("seq", 1))
        half = S((width // 2, part), f32)
        keep_a, send_a, keep_b, send_b = call(
            grads_kernel, [half] * 4, [left_a, left_b, own_a, came_a, own_b, came_b], f"grads_{r}",
            flops=8 * rows * width * part)
        next_a = lax.ppermute(send_a, "seq", flips("seq", 1))
        next_b = lax.ppermute(send_b, "seq", flips("seq", 0))
        halves.append(halving([jnp.stack([keep_a, keep_b]), jnp.stack([next_a, next_b])], order_hops))
    piece = S((rows, width // 2), f32)
    half_state = S((width // 2, 2 * state), f32)
    keep, send, state_keep, state_send = call(
        functools.partial(back_kernel, ROUNDS, s_order),
        [piece, piece, half_state, half_state],
        [ids] + grads + sums + [w_inner, w_state, ordered], "back",
        scratch=[pltpu.VMEM((width, 2 * state), f32)],
        flops=2 * rows * width * inner)
    came = lax.ppermute(send, "heads", flips("heads", 0))
    d_tokens = call(place_kernel, [S((rows, width // 2), bf16)], [ids, node_order, keep, came], "place",
                    flops=rows * rows * width)[0]
    came_state = lax.ppermute(state_send, "heads", flips("heads", 0))
    d_w_state = halving([state_keep, came_state], s_hops[1:])
    block = width // (n_order * n_seq)
    both = jnp.stack(halves)
    swap_a = lax.ppermute(both[:, 0, block:], "seq", flips("seq", 0))
    swap_b = lax.ppermute(both[:, 1, block:], "seq", flips("seq", 1))
    own = both[:, :, :block]
    swapped = jnp.stack([swap_a, swap_b], axis=1)
    flag = jnp.stack([role_a, role_b])[None, :, None, None] == 0
    inner_blocks = jnp.where(flag, own, swapped)
    out_blocks = jnp.where(flag, swapped, own)
    d_w_inner = inner_blocks.transpose(2, 0, 1, 3).reshape(block, inner)
    d_w_out = out_blocks.transpose(2, 0, 1, 3).reshape(block, inner)
    return d_tokens[None], d_w_inner, d_w_state, d_w_out


def solution(mesh):
    in_specs = (
        P("seq", "order", None),
        P("seq", "order", None),
        P("seq", "order"),
        P("seq", "order", "heads"),
        P(None, "heads"),
        P(),
        P(None, "heads"),
    )
    out_specs = (
        P("seq", "order", "heads"),
        P(("order", "seq"), "heads"),
        P(("order", "heads", "seq"), None),
        P(("order", "seq"), "heads"),
    )
    return jax.shard_map(
        per_device, mesh=mesh, in_specs=in_specs, out_specs=out_specs, check_vma=False
    )
```

```python
import functools

import jax
import jax.numpy as jnp
from jax import lax
from jax.experimental import pallas as pl
from jax.experimental.pallas import tpu as pltpu
from jax.sharding import PartitionSpec as P

CHUNK = 128
SHARES = (1, 1, 1, 1)
LIMIT = 24 * 1024 * 1024
LARGE = 60 * 1024 * 1024
SMALL = 16 * 1024 * 1024
f32 = jnp.float32
bf16 = jnp.bfloat16


def dot(a, b, ca=1, cb=0):
    return lax.dot_general(a, b, (((ca,), (cb,)), ((), ())), preferred_element_type=f32)


def log2(n):
    bits = n.bit_length() - 1
    assert 1 << bits == n
    return bits


def place(index, order):
    out = 0
    for rank, bit in enumerate(order):
        out = out + (((index >> bit) & 1) << (len(order) - 1 - rank))
    return out


def spread(values, first, heads, size):
    total = values.shape[0]
    row = lax.broadcasted_iota(jnp.int32, (total, heads * size), 0)
    col = lax.broadcasted_iota(jnp.int32, (total, heads * size), 1)
    low = (row - first) * size
    pick = jnp.where((col >= low) & (col < low + size), 1.0, 0.0).astype(bf16)
    high = values.astype(bf16)
    rest = values - high.astype(f32)
    middle = rest.astype(bf16)
    last = (rest - middle.astype(f32)).astype(bf16)
    return dot(high, pick, 0, 0) + dot(middle, pick, 0, 0) + dot(last, pick, 0, 0)


def triangle(upper):
    row = lax.broadcasted_iota(jnp.int32, (CHUNK, CHUNK), 0)
    col = lax.broadcasted_iota(jnp.int32, (CHUNK, CHUNK), 1)
    return row <= col if upper else row >= col


def one_hot_rows(offsets, rows):
    node = lax.broadcasted_iota(jnp.int32, (rows, offsets.shape[1]), 0)
    return jnp.where(node == offsets, 1.0, 0.0).astype(bf16)


def chunk_rows(cum_x, k):
    part = cum_x[k * CHUNK:(k + 1) * CHUNK]
    return part, part[CHUNK // 2 - 1:CHUNK // 2], part[CHUNK - 1:CHUNK]


def end_states(cum_x, x, dy, sc, sb, xs, ys, near):
    count = cum_x.shape[0] // CHUNK
    forward, back, decay = [], [], []
    for k in range(count):
        span = slice(k * CHUNK, (k + 1) * CHUNK)
        part, mid, last = chunk_rows(cum_x, k)
        x_s = (x[span] * jnp.exp(mid - part)).astype(bf16)
        y_s = (dy[span] * jnp.exp(part - mid)).astype(bf16)
        xs[span, :] = x_s
        ys[span, :] = y_s
        forward.append(jnp.exp(last - mid) * dot(sb[span, CHUNK:], x_s, 0, 0))
        back.append(jnp.exp(mid) * dot(sc[span, CHUNK:], y_s, 0, 0))
        decay.append(jnp.exp(last))
    run, run_back, factor = forward[0], back[-1], decay[0]
    for k in range(1, count):
        run = decay[k] * run + forward[k]
        factor = factor * decay[k]
        run_back = decay[count - 1 - k] * run_back + back[count - 1 - k]
    state = run.shape[0]
    near[:state, :] = run
    near[state:2 * state, :] = run_back
    near[2 * state:, :] = jnp.broadcast_to(factor, (8, factor.shape[1]))


def order_kernel(firsts, counts, size, ids, off, decays, *refs):
    sources, refs = refs[:5], refs[5:]
    outs = len(refs) // 2 - 3
    targets, refs = refs[:outs], refs[outs:]
    (tokens_v, cot_v, state_v, inner_v, out_v), refs = refs[:5], refs[5:]
    held, sems = refs[:outs], refs[outs]
    ordered, ordered_grad, early, sc, sb, cum = held[:6]
    loads = [pltpu.make_async_copy(source, target, sems.at[i])
             for i, (source, target) in enumerate(zip(sources, (tokens_v, cot_v, state_v, inner_v, out_v)))]
    stores = [pltpu.make_async_copy(source, target, sems.at[5 + i]) for i, (source, target) in enumerate(zip(held, targets))]
    for load in loads:
        load.start()
    base, role = ids[1], ids[4]
    rows = tokens_v.shape[0]
    hot = one_hot_rows(off[...] - base, rows)
    lower = triangle(False)
    upper = triangle(True)
    ones = jnp.where(upper, 1.0, 0.0)
    rates = jnp.log(decays[...])
    for k in range(rows // CHUNK):
        span = slice(k * CHUNK, (k + 1) * CHUNK)
        cum[:, span] = jnp.dot(rates[:, span], ones, precision=lax.Precision.HIGHEST, preferred_element_type=f32)
    stores[5].start()
    loads[0].wait()
    ordered[...] = dot(hot, tokens_v[...], 0, 0).astype(bf16)
    stores[0].start()
    loads[1].wait()
    ordered_grad[...] = dot(hot, cot_v[...], 0, 0).astype(bf16)
    stores[1].start()
    early[...] = jnp.where(role == 0, ordered_grad[...].astype(f32), ordered[...].astype(f32))
    stores[2].start()
    loads[2].wait()
    bc = dot(ordered[...], state_v[...]).astype(bf16)
    state = bc.shape[1] // 2
    for k in range(rows // CHUNK):
        span = slice(k * CHUNK, (k + 1) * CHUNK)
        b, c = bc[span, :state], bc[span, state:]
        sc[span, :CHUNK] = jnp.where(lower, dot(c, b, 1, 1), 0.0).astype(bf16)
        sc[span, CHUNK:] = c
        sb[span, :CHUNK] = jnp.where(upper, dot(b, c, 1, 1), 0.0).astype(bf16)
        sb[span, CHUNK:] = b
    stores[3].start()
    stores[4].start()
    loads[3].wait()
    loads[4].wait()
    for r, (first, heads) in enumerate(zip(firsts, counts)):
        cut = slice(first * size, (first + heads) * size)
        cum_x = spread(cum[...], first, heads, size)
        x = dot(ordered[...], inner_v[:, cut]).astype(bf16).astype(f32)
        dy = dot(ordered_grad[...], out_v[:, cut]).astype(bf16).astype(f32)
        end_states(cum_x, x, dy, sc, sb, *held[6 + 3 * r:9 + 3 * r])
        for i in range(6 + 3 * r, 9 + 3 * r):
            stores[i].start()
    for store in stores:
        store.wait()


def join_kernel(ids, near, came, out):
    state = out.shape[0]
    lower, odd = ids[5] < 2, ids[5] & 1 == 1
    own = jnp.where(lower, near[:state, :], near[state:2 * state, :])
    other = jnp.where(lower, came[:state, :], came[state:2 * state, :])
    out[...] = jnp.where(odd == lower, own + near[2 * state:2 * state + 1, :] * other,
                         other + came[2 * state:2 * state + 1, :] * own)


def turn_kernel(orders, ids, ordered, ordered_grad, near, left):
    me, side, role = ids[0], ids[2], ids[4]
    rows, width = ordered.shape
    half = width // 2
    blocks = 1 << len(orders[0])
    size = width // blocks
    for part in range(2):
        span = slice(part * half, (part + 1) * half)
        own = jnp.where(role == 0, ordered[:, span].astype(f32), ordered_grad[:, span].astype(f32)).astype(bf16)
        value = jnp.concatenate([own.T, near[:, span].astype(bf16).T], axis=1)
        for block in range(blocks // 2):
            index = (block + part * (blocks // 2)) ^ me
            where = jnp.where(side == 0, place(index, orders[0]), place(index, orders[1]))
            left[pl.ds(pl.multiple_of(where * size, size), size), :] = value[block * size:(block + 1) * size]


def outputs_kernel(first, heads, size, pieces, ready, ids, xs, ys, sc, sb, cum, came, *refs):
    far = None if ready else refs[0]
    refs = refs if ready else refs[1:]
    owns, sends, (grad_x, grad_bc) = refs[:pieces], refs[pieces:2 * pieces], refs[2 * pieces:]
    cum_x = spread(cum[...], first, heads, size)
    count = cum_x.shape[0] // CHUNK
    lower = triangle(False)
    upper = triangle(True)
    role = ids[4]
    state = (came.shape[0] - 8) // 2
    before, after = came[:state, :], came[state:2 * state, :]
    if not ready:
        factor = came[2 * state:2 * state + 1, :]
        first_half, odd = ids[5] < 2, ids[5] & 1 == 1
        before, after = (
            jnp.where(odd, before + jnp.where(first_half, 0.0, factor * far[...]), jnp.where(first_half, 0.0, far[...])),
            jnp.where(odd, jnp.where(first_half, far[...], 0.0), after + jnp.where(first_half, factor * far[...], 0.0)))
    starts, afters = [before], [after]
    for k in range(count - 1):
        span = slice(k * CHUNK, (k + 1) * CHUNK)
        _, mid, last = chunk_rows(cum_x, k)
        starts.append(jnp.exp(last) * starts[-1] + jnp.exp(last - mid) * dot(sb[span, CHUNK:], xs[span, :], 0, 0))
    for k in range(count - 1, 0, -1):
        span = slice(k * CHUNK, (k + 1) * CHUNK)
        _, mid, last = chunk_rows(cum_x, k)
        afters.insert(0, jnp.exp(last) * afters[0] + jnp.exp(mid) * dot(sc[span, CHUNK:], ys[span, :], 0, 0))
    for k in range(count):
        span = slice(k * CHUNK, (k + 1) * CHUNK)
        part, mid, last = chunk_rows(cum_x, k)
        x_s, y_s = xs[span, :], ys[span, :]
        x_rows = jnp.concatenate([x_s, (starts[k] * jnp.exp(mid)).astype(bf16)], axis=0)
        y_rows = jnp.concatenate([y_s, (afters[k] * jnp.exp(last - mid)).astype(bf16)], axis=0)
        y = (jnp.exp(part - mid) * dot(sc[span, :], x_rows)).astype(bf16)
        dx = (jnp.exp(mid - part) * dot(sb[span, :], y_rows)).astype(bf16)
        grad_x[span, :] = dx
        y, dx = y.astype(f32), dx.astype(f32)
        for i, (own, send) in enumerate(zip(owns, sends)):
            cut = slice(i * own.shape[1], (i + 1) * own.shape[1])
            own[span, :] = jnp.where(role == 0, dx[:, cut], y[:, cut]).astype(bf16)
            send[span, :] = jnp.where(role == 0, y[:, cut], dx[:, cut])
        by_y = dot(y_s, x_rows, 1, 1)
        by_x = dot(x_s, y_rows, 1, 1)
        pairs = jnp.where(lower, by_y[:, :CHUNK], 0.0).astype(bf16)
        turned = jnp.where(upper, by_x[:, :CHUNK], 0.0).astype(bf16)
        grad_bc[span, :state] = dot(turned, sc[span, CHUNK:]) + by_x[:, CHUNK:]
        grad_bc[span, state:] = dot(pairs, sb[span, CHUNK:]) + by_y[:, CHUNK:]


def grads_kernel(left, own, came, keep, send):
    half = left.shape[0] // 2
    right = jnp.concatenate([own[...], came[...].astype(bf16)], axis=0)
    send[...] = dot(left[half:, :], right)
    keep[...] = dot(left[:half, :], right)


def back_kernel(rounds, s_order, ids, *refs):
    grads, sums = refs[:rounds], refs[rounds:2 * rounds]
    w_inner, w_state, ordered, keep, state_keep, send, table = refs[2 * rounds:]
    side, me_state = ids[2], ids[3]
    grad_bc = sums[0][...]
    for part in sums[1:]:
        grad_bc = grad_bc + part[...]
    grad_bc = grad_bc.astype(bf16)
    width = ordered.shape[1]
    half = width // 2
    for out, which in ((send, 1 - side), (keep, side)):
        rows = pl.ds(pl.multiple_of(which * half, half), half)
        value = dot(grad_bc, w_state[rows, :], 1, 1)
        start = 0
        for part in grads:
            cols = part.shape[1]
            value = value + dot(part[...], w_inner[rows, start:start + cols], 1, 1)
            start += cols
        out[:, :half] = value
    fine = width >> len(s_order)
    step = width // 4
    for quarter in range(4):
        value = dot(ordered[:, quarter * step:(quarter + 1) * step], grad_bc, 0, 0)
        for piece in range(step // fine):
            index = (quarter * step) // fine + piece
            where = place(index ^ me_state, s_order)
            table[pl.ds(pl.multiple_of(where * fine, fine), fine), :] = value[piece * fine:(piece + 1) * fine]
    state_keep[...] = table[:half, :]
    send[:, half:] = table[half:, :]


def place_kernel(ids, off, keep, came, out):
    hot = one_hot_rows(off[...] - ids[1], out.shape[0])
    out[...] = dot(hot, (keep[...] + came[:, :keep.shape[1]]).astype(bf16)).astype(bf16)


def finish_kernel(rounds, ids, *refs):
    halves, (swap, d_inner, d_out) = refs[:rounds], refs[rounds:]
    block = d_inner.shape[0]
    start = 0
    for half in halves:
        cut = slice(start, start + half.shape[1])
        own, other = half[:block, :], swap[:, cut]
        d_inner[:, cut] = jnp.where(ids[4] == 0, own, other)
        d_out[:, cut] = jnp.where(ids[4] == 0, other, own)
        start += half.shape[1]


def flips(axis, bit):
    return [(i, i ^ (1 << bit)) for i in range(lax.axis_size(axis))]


def cross(value, bits):
    count = lax.axis_size("seq")
    pairs = [(h * count + s, h * count + (s ^ (1 << bit))) for h, bit in enumerate(bits) for s in range(count)]
    return lax.ppermute(value, ("heads", "seq"), pairs)


def total_of(parts, start, stop):
    out = parts[0][start:stop]
    for part in parts[1:]:
        out = out + part[start:stop]
    return out


def chain(near):
    count, mine = lax.axis_size("order"), lax.axis_index("order")
    state = (near.shape[0] - 8) // 2
    forward, back, total = near[:state], near[state:2 * state], near[2 * state:2 * state + 1]
    run, run_back = jnp.zeros_like(forward), jnp.zeros_like(back)
    for k in range(1, count):
        up = lax.ppermute(total * run + forward, "order", [(k - 1, k)])
        down = lax.ppermute(total * run_back + back, "order", [(count - k, count - k - 1)])
        run = jnp.where(mine == k, up, run)
        run_back = jnp.where(mine == count - k - 1, down, run_back)
    return jnp.concatenate([run, run_back, jnp.zeros_like(near[2 * state:])], axis=0)


class Line:
    def __init__(self, value):
        self.last = value

    def tie(self, *values):
        out = lax.optimization_barrier((self.last,) + values)
        self.last = out[0]
        return out[1:] if len(values) > 1 else out[1]

    def did(self, value):
        self.last = value


class Sum:
    def __init__(self, line, parts, hops):
        self.line, self.parts, self.hops = line, parts, list(hops)

    def hop(self):
        axis, bit = self.hops.pop(0)
        rows = self.parts[0].shape[0] // 2
        tied = self.line.tie(*self.parts)
        message = total_of(tied, rows, 2 * rows)
        self.line.did(message)
        self.parts = [p[:rows] for p in tied] + [lax.ppermute(message, axis, flips(axis, bit))]

    def result(self):
        return total_of(self.parts, 0, self.parts[0].shape[0])


def whole(array):
    return pl.BlockSpec(array.shape, lambda *_: (0,) * len(array.shape))


def call(kernel, outs, args, name, scratch=(), specs=None, limit=LIMIT, out_specs=None):
    specs = specs or {}
    out_specs = out_specs or {}
    in_specs = []
    for i, arg in enumerate(args):
        if i in specs:
            in_specs.append(specs[i])
        elif arg.dtype == jnp.int32 and arg.ndim == 1:
            in_specs.append(pl.BlockSpec(memory_space=pltpu.SMEM))
        else:
            in_specs.append(whole(arg))
    return pl.pallas_call(
        kernel,
        out_shape=tuple(outs),
        grid=(1,),
        in_specs=in_specs,
        out_specs=tuple(out_specs.get(i, whole(o)) for i, o in enumerate(outs)),
        scratch_shapes=list(scratch),
        compiler_params=pltpu.CompilerParams(vmem_limit_bytes=limit),
        cost_estimate=pl.CostEstimate(flops=16_000_000_000, bytes_accessed=1000, transcendentals=0),
        name=name,
    )(*args)


def per_device(tokens, cotangent, node_order, decays, w_inner, w_state, w_out):
    assert tokens.shape[0] == 1
    tokens, cotangent, decays = tokens[0], cotangent[0], decays[0]
    rows, width = tokens.shape
    heads = decays.shape[1]
    inner = w_inner.shape[1]
    size = inner // heads
    state = w_state.shape[1] // 2
    unit = heads // sum(SHARES)
    firsts = [unit * sum(SHARES[:r]) for r in range(len(SHARES))]
    counts = [unit * share for share in SHARES]
    n_order, n_heads, n_seq = (lax.axis_size(a) for a in ("order", "heads", "seq"))
    o, h, s = (lax.axis_index(a) for a in ("order", "heads", "seq"))
    seq_bits, head_bits, order_bits = log2(n_seq), log2(n_heads), log2(n_order)
    assert seq_bits == 2 and head_bits == 1
    order_hops = [("order", b) for b in range(order_bits)]
    s_hops = [("heads", 0)] + order_hops + [("seq", 0), ("seq", 1)]
    shift_state = {"seq": 0, "heads": seq_bits, "order": seq_bits + head_bits}
    s_order = [shift_state[a] + b for a, b in s_hops]
    pair_bits, sum_bits = (0, 1), (1, 0)
    orders = [[sum_bits[c]] + [seq_bits + b for b in range(order_bits)] + [pair_bits[c]] for c in range(2)]
    role = jnp.where(h == 0, s & 1, (s >> 1) & 1)
    ids = jnp.stack([o * n_seq + s, o * rows, h, (o * n_heads + h) * n_seq + s, role, o]).astype(jnp.int32)
    S = jax.ShapeDtypeStruct
    full = S((rows, width), bf16)
    sent = S((rows, width), f32)
    wide = S((rows, CHUNK + state), bf16)
    far_space = pl.BlockSpec(memory_space=pltpu.HBM)

    outs = [full, full, sent, wide, wide, S((heads, rows), f32)]
    for count in counts:
        outs += [S((rows, count * size), bf16)] * 2 + [S((2 * state + 8, count * size), f32)]
    order_args = [ids, node_order, decays.T, tokens, cotangent, w_state, w_inner, w_out]
    made = call(
        functools.partial(order_kernel, firsts, counts, size), outs, order_args, "order",
        specs={i: far_space for i in range(3, 8)}, out_specs={i: far_space for i in range(len(outs))},
        scratch=[pltpu.VMEM(a.shape, a.dtype) for a in order_args[3:] + outs] + [pltpu.SemaphoreType.DMA((5 + len(outs),))],
        limit=LARGE)
    ordered, ordered_grad, early, sc, sb, cum = made[:6]
    count_rounds = len(SHARES)
    line = Line(ids)
    tree = n_order == 4
    nears = {0: lax.ppermute(made[8], "order", flips("order", 0)) if tree else chain(made[8])}
    near_tokens = cross(early, pair_bits)
    incoming, owns, swapped, grads, sums, halves = {}, {}, {}, {}, {}, {}
    held = {}

    def join(r):
        near = made[8 + 3 * r]
        if tree:
            came = nears[r]
            joined, = call(join_kernel, [S((state, near.shape[1]), f32)], [line.tie(ids), near, came], f"join_{r}")
            line.did(joined)
            incoming[r] = (came, lax.ppermute(joined, "order", flips("order", 1)))
            if r + 1 < count_rounds:
                following, _ = lax.optimization_barrier((made[11 + 3 * r], joined))
                nears[r + 1] = lax.ppermute(following, "order", flips("order", 0))
        else:
            incoming[r] = (nears[r],)
            if r + 1 < count_rounds:
                nears[r + 1] = chain(made[11 + 3 * r])

    def outputs(r):
        cols = counts[r] * size
        own, send, grads[r], sums[r] = call(
            functools.partial(outputs_kernel, firsts[r], counts[r], size, 1, not tree),
            [S((rows, cols), bf16), S((rows, cols), f32), S((rows, cols), bf16), S((rows, 2 * state), f32)],
            [line.tie(ids), *made[6 + 3 * r:8 + 3 * r], sc, sb, cum, *incoming[r]], f"outputs_{r}")
        line.did(send)
        owns[r], swapped[r] = own, cross(send, pair_bits)

    def turn():
        held["left"], = call(functools.partial(turn_kernel, orders), [S((width, 2 * rows), bf16)],
                             [line.tie(ids), ordered, ordered_grad, near_tokens], "turn")
        line.did(held["left"])

    def gradients(r):
        half = S((width // 2, counts[r] * size), f32)
        keep, send = call(grads_kernel, [half] * 2, [held["left"], line.tie(owns[r]), swapped[r]], f"grads_{r}")
        line.did(send)
        halves[r] = Sum(line, [keep, cross(send, sum_bits)], order_hops)

    def back():
        keep, state_keep, send = call(
            functools.partial(back_kernel, count_rounds, s_order),
            [S((rows, width // 2), f32), S((width // 2, 2 * state), f32), S((rows, width // 2 + 2 * state), f32)],
            [line.tie(ids)] + [grads[r] for r in range(count_rounds)] + [sums[r] for r in range(count_rounds)]
            + [w_inner, w_state, ordered], "back", scratch=[pltpu.VMEM((width, 2 * state), f32)])
        line.did(send)
        held["keep"], held["came"] = keep, lax.ppermute(send, "heads", flips("heads", 0))
        held["state"] = Sum(line, [state_keep, held["came"][:, width // 2:]], s_hops[1:])

    def place_rows():
        held["tokens"], = call(place_kernel, [S((rows, width // 2), bf16)],
                               [line.tie(ids), node_order, held["keep"], held["came"]], "place")
        line.did(held["tokens"])

    steps = [(8.0, turn), (8.5 * count_rounds - 8, back), (8.5 * count_rounds + 1, place_rows)]
    for r in range(count_rounds):
        start = 8.5 * r
        steps += [(start - 9.5, functools.partial(join, r)), (start, functools.partial(outputs, r)),
                  (start + 11, functools.partial(gradients, r))]
        steps += [(start + 23 + 8 * k, lambda r=r: halves[r].hop()) for k in range(order_bits)]
    steps += [(8.5 * count_rounds + 10 + 8 * k, lambda: held["state"].hop()) for k in range(order_bits)]
    for _, step in sorted(steps, key=lambda entry: entry[0]):
        step()
    halves = [halves[r].result() for r in range(count_rounds)]
    d_tokens = held["tokens"]
    while held["state"].hops:
        held["state"].hop()
    d_w_state = held["state"].result()
    block = width // (n_order * n_seq)
    swap = cross(jnp.concatenate([h[block:] for h in halves], axis=1), pair_bits)
    final = S((block, inner), f32)
    d_w_inner, d_w_out = call(functools.partial(finish_kernel, len(halves)), [final, final],
                              [ids] + halves + [swap], "finish", limit=SMALL)
    return d_tokens[None], d_w_inner, d_w_state, d_w_out


def solution(mesh):
    in_specs = (
        P("seq", "order", None),
        P("seq", "order", None),
        P("seq", "order"),
        P("seq", "order", "heads"),
        P(None, "heads"),
        P(),
        P(None, "heads"),
    )
    out_specs = (
        P("seq", "order", "heads"),
        P(("order", "seq"), "heads"),
        P(("order", "heads", "seq"), None),
        P(("order", "seq"), "heads"),
    )
    return jax.shard_map(
        per_device, mesh=mesh, in_specs=in_specs, out_specs=out_specs, check_vma=False
    )
```

```python
import functools

import jax
import jax.numpy as jnp
from jax import lax
from jax.experimental import pallas as pl
from jax.experimental.pallas import tpu as pltpu
from jax.sharding import PartitionSpec as P

CHUNK = 128
SHARES = (1, 1, 1, 1)
LIMIT = 24 * 1024 * 1024
LARGE = 60 * 1024 * 1024
HEAVY = 16_000_000_000
LIGHT = 16_000_000_000
SMALL = 16 * 1024 * 1024
f32 = jnp.float32
bf16 = jnp.bfloat16


def dot(a, b, ca=1, cb=0):
    return lax.dot_general(a, b, (((ca,), (cb,)), ((), ())), preferred_element_type=f32)


def log2(n):
    bits = n.bit_length() - 1
    assert 1 << bits == n
    return bits


def place(index, order):
    out = 0
    for rank, bit in enumerate(order):
        out = out + (((index >> bit) & 1) << (len(order) - 1 - rank))
    return out


def spread(values, first, heads, size):
    total = values.shape[0]
    row = lax.broadcasted_iota(jnp.int32, (total, heads * size), 0)
    col = lax.broadcasted_iota(jnp.int32, (total, heads * size), 1)
    low = (row - first) * size
    pick = jnp.where((col >= low) & (col < low + size), 1.0, 0.0).astype(bf16)
    high = values.astype(bf16)
    rest = values - high.astype(f32)
    middle = rest.astype(bf16)
    last = (rest - middle.astype(f32)).astype(bf16)
    return dot(high, pick, 0, 0) + dot(middle, pick, 0, 0) + dot(last, pick, 0, 0)


def triangle(upper):
    row = lax.broadcasted_iota(jnp.int32, (CHUNK, CHUNK), 0)
    col = lax.broadcasted_iota(jnp.int32, (CHUNK, CHUNK), 1)
    return row <= col if upper else row >= col


def one_hot_rows(offsets, rows):
    node = lax.broadcasted_iota(jnp.int32, (rows, offsets.shape[1]), 0)
    return jnp.where(node == offsets, 1.0, 0.0).astype(bf16)


def chunk_rows(cum_x, k):
    part = cum_x[k * CHUNK:(k + 1) * CHUNK]
    return part, part[CHUNK // 2 - 1:CHUNK // 2], part[CHUNK - 1:CHUNK]


def end_states(cum_x, x, dy, sc, sb, xs, ys, near):
    count = cum_x.shape[0] // CHUNK
    forward, back, decay = [], [], []
    for k in range(count):
        span = slice(k * CHUNK, (k + 1) * CHUNK)
        part, mid, last = chunk_rows(cum_x, k)
        x_s = (x[span] * jnp.exp(mid - part)).astype(bf16)
        y_s = (dy[span] * jnp.exp(part - mid)).astype(bf16)
        xs[span, :] = x_s
        ys[span, :] = y_s
        forward.append(jnp.exp(last - mid) * dot(sb[span, CHUNK:], x_s, 0, 0))
        back.append(jnp.exp(mid) * dot(sc[span, CHUNK:], y_s, 0, 0))
        decay.append(jnp.exp(last))
    run, run_back, factor = forward[0], back[-1], decay[0]
    for k in range(1, count):
        run = decay[k] * run + forward[k]
        factor = factor * decay[k]
        run_back = decay[count - 1 - k] * run_back + back[count - 1 - k]
    state = run.shape[0]
    near[:state, :] = run
    near[state:2 * state, :] = run_back
    near[2 * state:, :] = jnp.broadcast_to(factor, (8, factor.shape[1]))


def order_kernel(heads, size, ids, off, decays, *refs):
    sources, refs = refs[:5], refs[5:]
    outs = len(refs) // 2 - 3
    targets, refs = refs[:outs], refs[outs:]
    (tokens_v, cot_v, state_v, inner_v, out_v), refs = refs[:5], refs[5:]
    held, sems = refs[:outs], refs[outs]
    ordered, ordered_grad, early, sc, sb, cum = held[:6]
    cut = pl.ds(0, heads * size)
    sources = [*sources[:3], sources[3].at[:, cut], sources[4].at[:, cut]]
    loads = [pltpu.make_async_copy(source, target, sems.at[i])
             for i, (source, target) in enumerate(zip(sources, (tokens_v, cot_v, state_v, inner_v, out_v)))]
    stores = [pltpu.make_async_copy(source, target, sems.at[5 + i]) for i, (source, target) in enumerate(zip(held, targets))]
    for load in loads:
        load.start()
    base, role = ids[1], ids[4]
    rows = tokens_v.shape[0]
    hot = one_hot_rows(off[...] - base, rows)
    lower = triangle(False)
    upper = triangle(True)
    ones = jnp.where(upper, 1.0, 0.0)
    rates = jnp.log(decays[...])
    for k in range(rows // CHUNK):
        span = slice(k * CHUNK, (k + 1) * CHUNK)
        cum[:, span] = jnp.dot(rates[:, span], ones, precision=lax.Precision.HIGHEST, preferred_element_type=f32)
    stores[5].start()
    loads[0].wait()
    ordered[...] = dot(hot, tokens_v[...], 0, 0).astype(bf16)
    stores[0].start()
    loads[1].wait()
    ordered_grad[...] = dot(hot, cot_v[...], 0, 0).astype(bf16)
    stores[1].start()
    early[...] = jnp.where(role == 0, ordered_grad[...].astype(f32), ordered[...].astype(f32))
    stores[2].start()
    loads[2].wait()
    bc = dot(ordered[...], state_v[...]).astype(bf16)
    state = bc.shape[1] // 2
    for k in range(rows // CHUNK):
        span = slice(k * CHUNK, (k + 1) * CHUNK)
        b, c = bc[span, :state], bc[span, state:]
        sc[span, :CHUNK] = jnp.where(lower, dot(c, b, 1, 1), 0.0).astype(bf16)
        sc[span, CHUNK:] = c
        sb[span, :CHUNK] = jnp.where(upper, dot(b, c, 1, 1), 0.0).astype(bf16)
        sb[span, CHUNK:] = b
    stores[3].start()
    stores[4].start()
    loads[3].wait()
    x = dot(ordered[...], inner_v[...]).astype(bf16).astype(f32)
    loads[4].wait()
    dy = dot(ordered_grad[...], out_v[...]).astype(bf16).astype(f32)
    end_states(spread(cum[...], 0, heads, size), x, dy, sc, sb, *held[6:9])
    for store in stores[6:]:
        store.start()
    for store in stores:
        store.wait()


def rest_kernel(firsts, counts, size, sc, sb, cum, *refs):
    sources, refs = refs[:4], refs[4:]
    outs = len(refs) // 2 - 2
    targets, refs = refs[:outs], refs[outs:]
    (ordered, ordered_grad, inner_v, out_v), refs = refs[:4], refs[4:]
    held, sems = refs[:outs], refs[outs]
    base = firsts[0] * size
    cut = pl.ds(base, inner_v.shape[1])
    sources = [sources[0], sources[1], sources[2].at[:, cut], sources[3].at[:, cut]]
    loads = [pltpu.make_async_copy(source, target, sems.at[i])
             for i, (source, target) in enumerate(zip(sources, (ordered, ordered_grad, inner_v, out_v)))]
    stores = [pltpu.make_async_copy(source, target, sems.at[4 + i]) for i, (source, target) in enumerate(zip(held, targets))]
    for load in loads:
        load.start()
    for load in loads:
        load.wait()
    for r, (first, heads) in enumerate(zip(firsts, counts)):
        cut = slice(first * size - base, (first + heads) * size - base)
        x = dot(ordered[...], inner_v[:, cut]).astype(bf16).astype(f32)
        dy = dot(ordered_grad[...], out_v[:, cut]).astype(bf16).astype(f32)
        end_states(spread(cum[...], first, heads, size), x, dy, sc, sb, *held[3 * r:3 * r + 3])
        for store in stores[3 * r:3 * r + 3]:
            store.start()
    for store in stores:
        store.wait()


def join_kernel(ids, near, came, out):
    state = out.shape[0]
    lower, odd = ids[5] < 2, ids[5] & 1 == 1
    own = jnp.where(lower, near[:state, :], near[state:2 * state, :])
    other = jnp.where(lower, came[:state, :], came[state:2 * state, :])
    out[...] = jnp.where(odd == lower, own + near[2 * state:2 * state + 1, :] * other,
                         other + came[2 * state:2 * state + 1, :] * own)


def turn_kernel(orders, ids, ordered, ordered_grad, near, left):
    me, side, role = ids[0], ids[2], ids[4]
    rows, width = ordered.shape
    half = width // 2
    blocks = 1 << len(orders[0])
    size = width // blocks
    for part in range(2):
        span = slice(part * half, (part + 1) * half)
        own = jnp.where(role == 0, ordered[:, span].astype(f32), ordered_grad[:, span].astype(f32)).astype(bf16)
        value = jnp.concatenate([own.T, near[:, span].astype(bf16).T], axis=1)
        for block in range(blocks // 2):
            index = (block + part * (blocks // 2)) ^ me
            where = jnp.where(side == 0, place(index, orders[0]), place(index, orders[1]))
            left[pl.ds(pl.multiple_of(where * size, size), size), :] = value[block * size:(block + 1) * size]


def outputs_kernel(first, heads, size, pieces, ready, ids, xs, ys, sc, sb, cum, came, *refs):
    far = None if ready else refs[0]
    refs = refs if ready else refs[1:]
    owns, sends, (grad_x, grad_bc) = refs[:pieces], refs[pieces:2 * pieces], refs[2 * pieces:]
    cum_x = spread(cum[...], first, heads, size)
    count = cum_x.shape[0] // CHUNK
    lower = triangle(False)
    upper = triangle(True)
    role = ids[4]
    state = (came.shape[0] - 8) // 2
    before, after = came[:state, :], came[state:2 * state, :]
    if not ready:
        factor = came[2 * state:2 * state + 1, :]
        first_half, odd = ids[5] < 2, ids[5] & 1 == 1
        before, after = (
            jnp.where(odd, before + jnp.where(first_half, 0.0, factor * far[...]), jnp.where(first_half, 0.0, far[...])),
            jnp.where(odd, jnp.where(first_half, far[...], 0.0), after + jnp.where(first_half, factor * far[...], 0.0)))
    starts, afters = [before], [after]
    for k in range(count - 1):
        span = slice(k * CHUNK, (k + 1) * CHUNK)
        _, mid, last = chunk_rows(cum_x, k)
        starts.append(jnp.exp(last) * starts[-1] + jnp.exp(last - mid) * dot(sb[span, CHUNK:], xs[span, :], 0, 0))
    for k in range(count - 1, 0, -1):
        span = slice(k * CHUNK, (k + 1) * CHUNK)
        _, mid, last = chunk_rows(cum_x, k)
        afters.insert(0, jnp.exp(last) * afters[0] + jnp.exp(mid) * dot(sc[span, CHUNK:], ys[span, :], 0, 0))
    for k in range(count):
        span = slice(k * CHUNK, (k + 1) * CHUNK)
        part, mid, last = chunk_rows(cum_x, k)
        x_s, y_s = xs[span, :], ys[span, :]
        x_rows = jnp.concatenate([x_s, (starts[k] * jnp.exp(mid)).astype(bf16)], axis=0)
        y_rows = jnp.concatenate([y_s, (afters[k] * jnp.exp(last - mid)).astype(bf16)], axis=0)
        y = (jnp.exp(part - mid) * dot(sc[span, :], x_rows)).astype(bf16)
        dx = (jnp.exp(mid - part) * dot(sb[span, :], y_rows)).astype(bf16)
        grad_x[span, :] = dx
        y, dx = y.astype(f32), dx.astype(f32)
        for i, (own, send) in enumerate(zip(owns, sends)):
            cut = slice(i * own.shape[1], (i + 1) * own.shape[1])
            own[span, :] = jnp.where(role == 0, dx[:, cut], y[:, cut]).astype(bf16)
            send[span, :] = jnp.where(role == 0, y[:, cut], dx[:, cut])
        by_y = dot(y_s, x_rows, 1, 1)
        by_x = dot(x_s, y_rows, 1, 1)
        pairs = jnp.where(lower, by_y[:, :CHUNK], 0.0).astype(bf16)
        turned = jnp.where(upper, by_x[:, :CHUNK], 0.0).astype(bf16)
        grad_bc[span, :state] = dot(turned, sc[span, CHUNK:]) + by_x[:, CHUNK:]
        grad_bc[span, state:] = dot(pairs, sb[span, CHUNK:]) + by_y[:, CHUNK:]


def grads_kernel(left, own, came, keep, send):
    half = left.shape[0] // 2
    right = jnp.concatenate([own[...], came[...].astype(bf16)], axis=0)
    send[...] = dot(left[half:, :], right)
    keep[...] = dot(left[:half, :], right)


def back_kernel(rounds, s_orders, ids, *refs):
    grads, sums = refs[:rounds], refs[rounds:2 * rounds]
    w_inner, w_state, ordered, keep, state_keep, send, table = refs[2 * rounds:]
    side, me_state = ids[2], ids[3]
    grad_bc = sums[0][...]
    for part in sums[1:]:
        grad_bc = grad_bc + part[...]
    grad_bc = grad_bc.astype(bf16)
    width = ordered.shape[1]
    half = width // 2
    for out, which in ((send, 1 - side), (keep, side)):
        rows = pl.ds(pl.multiple_of(which * half, half), half)
        value = dot(grad_bc, w_state[rows, :], 1, 1)
        start = 0
        for part in grads:
            cols = part.shape[1]
            value = value + dot(part[...], w_inner[rows, start:start + cols], 1, 1)
            start += cols
        out[:, :half] = value
    fine = width >> len(s_orders[0])
    step = width // 4
    for quarter in range(4):
        value = dot(ordered[:, quarter * step:(quarter + 1) * step], grad_bc, 0, 0)
        for piece in range(step // fine):
            index = (quarter * step) // fine + piece
            index = index ^ me_state
            owner = side ^ ((index >> s_orders[0][0]) & 1)
            where = jnp.where(owner == 0, place(index, s_orders[0]), place(index, s_orders[1]))
            table[pl.ds(pl.multiple_of(where * fine, fine), fine), :] = value[piece * fine:(piece + 1) * fine]
    state_keep[...] = table[:half, :]
    send[:, half:] = table[half:, :]


def place_kernel(ids, off, keep, came, out):
    hot = one_hot_rows(off[...] - ids[1], out.shape[0])
    out[...] = dot(hot, (keep[...] + came[:, :keep.shape[1]]).astype(bf16)).astype(bf16)


def finish_kernel(rounds, ids, *refs):
    halves, (state, most, last, d_inner, d_out, d_state) = refs[:rounds], refs[rounds:]
    block, fine = d_inner.shape[0], d_state.shape[0]
    start = 0
    for r, half in enumerate(halves):
        cut = slice(start, start + half.shape[1])
        own, other = half[:block, :], most[:, cut] if r + 1 < rounds else last[:block, :]
        d_inner[:, cut] = jnp.where(ids[4] == 0, own, other)
        d_out[:, cut] = jnp.where(ids[4] == 0, other, own)
        start += half.shape[1]
    d_state[...] = state[:fine, :] + last[block:, :]


def flips(axis, bit):
    return [(i, i ^ (1 << bit)) for i in range(lax.axis_size(axis))]


def cross(value, bits):
    count = lax.axis_size("seq")
    pairs = [(h * count + s, h * count + (s ^ (1 << bit))) for h, bit in enumerate(bits) for s in range(count)]
    return lax.ppermute(value, ("heads", "seq"), pairs)


def total_of(parts, start, stop):
    out = parts[0][start:stop]
    for part in parts[1:]:
        out = out + part[start:stop]
    return out


def chain(near):
    count, mine = lax.axis_size("order"), lax.axis_index("order")
    state = (near.shape[0] - 8) // 2
    forward, back, total = near[:state], near[state:2 * state], near[2 * state:2 * state + 1]
    run, run_back = jnp.zeros_like(forward), jnp.zeros_like(back)
    for k in range(1, count):
        up = lax.ppermute(total * run + forward, "order", [(k - 1, k)])
        down = lax.ppermute(total * run_back + back, "order", [(count - k, count - k - 1)])
        run = jnp.where(mine == k, up, run)
        run_back = jnp.where(mine == count - k - 1, down, run_back)
    return jnp.concatenate([run, run_back, jnp.zeros_like(near[2 * state:])], axis=0)


class Line:
    def __init__(self, value):
        self.last = value

    def tie(self, *values):
        out = lax.optimization_barrier((self.last,) + values)
        self.last = out[0]
        return out[1:] if len(values) > 1 else out[1]

    def did(self, value):
        self.last = value


class Sum:
    def __init__(self, line, segments, hops):
        self.line, self.segments, self.hops = line, segments, list(hops)

    def hop(self):
        axis, bit = self.hops.pop(0)
        halves = [parts[0].shape[0] // 2 for parts in self.segments]
        flat = self.line.tie(*[part for parts in self.segments for part in parts])
        tied, start = [], 0
        for parts in self.segments:
            tied.append(flat[start:start + len(parts)])
            start += len(parts)
        message = rows_of([total_of(parts, half, 2 * half) for parts, half in zip(tied, halves)])
        self.line.did(message)
        came = lax.ppermute(message, axis, flips(axis, bit))
        start = 0
        self.segments = []
        for parts, half in zip(tied, halves):
            self.segments.append([p[:half] for p in parts] + [came[start:start + half]])
            start += half

    def result(self):
        return [total_of(parts, 0, parts[0].shape[0]) for parts in self.segments]


def rows_of(arrays):
    return arrays[0] if len(arrays) == 1 else jnp.concatenate(arrays, axis=0)


def whole(array):
    return pl.BlockSpec(array.shape, lambda *_: (0,) * len(array.shape))


def call(kernel, outs, args, name, scratch=(), specs=None, limit=LIMIT, out_specs=None, cost=LIGHT):
    specs = specs or {}
    out_specs = out_specs or {}
    in_specs = []
    for i, arg in enumerate(args):
        if i in specs:
            in_specs.append(specs[i])
        elif arg.dtype == jnp.int32 and arg.ndim == 1:
            in_specs.append(pl.BlockSpec(memory_space=pltpu.SMEM))
        else:
            in_specs.append(whole(arg))
    return pl.pallas_call(
        kernel,
        out_shape=tuple(outs),
        grid=(1,),
        in_specs=in_specs,
        out_specs=tuple(out_specs.get(i, whole(o)) for i, o in enumerate(outs)),
        scratch_shapes=list(scratch),
        compiler_params=pltpu.CompilerParams(vmem_limit_bytes=limit),
        cost_estimate=pl.CostEstimate(flops=cost, bytes_accessed=1000, transcendentals=0),
        name=name,
    )(*args)


def per_device(tokens, cotangent, node_order, decays, w_inner, w_state, w_out):
    assert tokens.shape[0] == 1
    tokens, cotangent, decays = tokens[0], cotangent[0], decays[0]
    rows, width = tokens.shape
    heads = decays.shape[1]
    inner = w_inner.shape[1]
    size = inner // heads
    state = w_state.shape[1] // 2
    unit = heads // sum(SHARES)
    firsts = [unit * sum(SHARES[:r]) for r in range(len(SHARES))]
    counts = [unit * share for share in SHARES]
    n_order, n_heads, n_seq = (lax.axis_size(a) for a in ("order", "heads", "seq"))
    o, h, s = (lax.axis_index(a) for a in ("order", "heads", "seq"))
    seq_bits, head_bits, order_bits = log2(n_seq), log2(n_heads), log2(n_order)
    assert seq_bits == 2 and head_bits == 1
    order_hops = [("order", b) for b in range(order_bits)]
    pair_bits, sum_bits = (0, 1), (1, 0)
    orders = [[sum_bits[c]] + [seq_bits + b for b in range(order_bits)] + [pair_bits[c]] for c in range(2)]
    s_orders = [[seq_bits, sum_bits[c]] + [seq_bits + 1 + b for b in range(order_bits)] + [pair_bits[c]] for c in range(2)]
    role = jnp.where(h == 0, s & 1, (s >> 1) & 1)
    ids = jnp.stack([o * n_seq + s, o * rows, h, (o * n_heads + h) * n_seq + s, role, o]).astype(jnp.int32)
    S = jax.ShapeDtypeStruct
    full = S((rows, width), bf16)
    sent = S((rows, width), f32)
    wide = S((rows, CHUNK + state), bf16)
    far_space = pl.BlockSpec(memory_space=pltpu.HBM)

    def ends(count):
        return [S((rows, count * size), bf16)] * 2 + [S((2 * state + 8, count * size), f32)]

    outs = [full, full, sent, wide, wide, S((heads, rows), f32)] + ends(counts[0])
    order_args = [ids, node_order, decays.T, tokens, cotangent, w_state, w_inner, w_out]
    cols = counts[0] * size
    made = call(
        functools.partial(order_kernel, counts[0], size), outs, order_args, "order",
        specs={i: far_space for i in range(3, 8)}, out_specs={i: far_space for i in range(len(outs))},
        scratch=[pltpu.VMEM(a.shape, a.dtype) for a in order_args[3:6]] + [pltpu.VMEM((width, cols), bf16)] * 2
        + [pltpu.VMEM(a.shape, a.dtype) for a in outs] + [pltpu.SemaphoreType.DMA((5 + len(outs),))],
        limit=LARGE, cost=HEAVY)
    ordered, ordered_grad, early, sc, sb, cum = made[:6]
    near_first = lax.ppermute(made[8], "order", flips("order", 0)) if n_order == 4 else chain(made[8])
    near_tokens = cross(early, pair_bits)
    outs = [out for count in counts[1:] for out in ends(count)]
    made += call(
        functools.partial(rest_kernel, firsts[1:], counts[1:], size), outs,
        [sc, sb, cum, ordered, ordered_grad, w_inner, w_out], "rest",
        specs={i: far_space for i in range(3, 7)}, out_specs={i: far_space for i in range(len(outs))},
        scratch=[pltpu.VMEM((rows, width), bf16)] * 2 + [pltpu.VMEM((width, inner - cols), bf16)] * 2
        + [pltpu.VMEM(a.shape, a.dtype) for a in outs] + [pltpu.SemaphoreType.DMA((4 + len(outs),))],
        limit=LARGE, cost=HEAVY)
    count_rounds = len(SHARES)
    block = width // (n_order * n_seq)
    fine = block // n_heads
    line = Line(ids)
    tree = n_order == 4
    nears = {0: near_first}
    line.did(made[11])
    incoming, owns, swapped, grads, sums, halves = {}, {}, {}, {}, {}, {}
    held = {}

    def join(r):
        near = made[8 + 3 * r]
        if tree:
            came = nears[r]
            joined, = call(join_kernel, [S((state, near.shape[1]), f32)], [line.tie(ids), near, came], f"join_{r}")
            line.did(joined)
            incoming[r] = (came, lax.ppermute(joined, "order", flips("order", 1)))
            if r + 1 < count_rounds:
                following, _ = lax.optimization_barrier((made[11 + 3 * r], joined))
                nears[r + 1] = lax.ppermute(following, "order", flips("order", 0))
        else:
            incoming[r] = (nears[r],)
            if r + 1 < count_rounds:
                nears[r + 1] = chain(made[11 + 3 * r])

    def outputs(r):
        cols = counts[r] * size
        own, send, grads[r], sums[r] = call(
            functools.partial(outputs_kernel, firsts[r], counts[r], size, 1, not tree),
            [S((rows, cols), bf16), S((rows, cols), f32), S((rows, cols), bf16), S((rows, 2 * state), f32)],
            [line.tie(ids), *made[6 + 3 * r:8 + 3 * r], sc, sb, cum, *incoming[r]], f"outputs_{r}", cost=HEAVY)
        line.did(send)
        owns[r], swapped[r] = own, cross(send, pair_bits)

    def turn():
        held["left"], = call(functools.partial(turn_kernel, orders), [S((width, 2 * rows), bf16)],
                             [line.tie(ids), ordered, ordered_grad, near_tokens], "turn")
        line.did(held["left"])

    def gradients(r):
        half = S((width // 2, counts[r] * size), f32)
        keep, send = call(grads_kernel, [half] * 2, [held["left"], line.tie(owns[r]), swapped[r]], f"grads_{r}")
        line.did(send)
        segments = [[keep]]
        if r == count_rounds - 1:
            whole_state = held["state"]
            middle = whole_state[0].shape[0] // 2
            send = rows_of([send, total_of(whole_state, middle, 2 * middle)])
            segments.append([part[:middle] for part in whole_state])
        came, start = cross(send, sum_bits), 0
        for parts in segments:
            parts.append(came[start:start + parts[0].shape[0]])
            start += parts[0].shape[0]
        halves[r] = Sum(line, segments, order_hops)

    def back():
        keep, state_keep, send = call(
            functools.partial(back_kernel, count_rounds, s_orders),
            [S((rows, width // 2), f32), S((width // 2, 2 * state), f32), S((rows, width // 2 + 2 * state), f32)],
            [line.tie(ids)] + [grads[r] for r in range(count_rounds)] + [sums[r] for r in range(count_rounds)]
            + [w_inner, w_state, ordered], "back", scratch=[pltpu.VMEM((width, 2 * state), f32)])
        line.did(send)
        held["keep"], held["came"] = keep, lax.ppermute(send, "heads", flips("heads", 0))
        held["state"] = [state_keep, held["came"][:, width // 2:]]

    def place_rows():
        held["tokens"], = call(place_kernel, [S((rows, width // 2), bf16)],
                               [line.tie(ids), node_order, held["keep"], held["came"]], "place")
        line.did(held["tokens"])

    def swap_most():
        held["most"] = [halves[r].result()[0] for r in range(count_rounds - 1)]
        message = jnp.concatenate([line.tie(h)[block:] for h in held["most"]], axis=1)
        line.did(message)
        held["swap"] = cross(message, pair_bits)

    steps = [(8.0, turn), (8.5 * count_rounds - 8, back), (8.5 * count_rounds + 1, place_rows)]
    for r in range(count_rounds):
        start = 8.5 * r
        steps += [(start - 9.5, functools.partial(join, r)), (start, functools.partial(outputs, r)),
                  (start + 11, functools.partial(gradients, r))]
        steps += [(start + 23 + 8 * k, lambda r=r: halves[r].hop()) for k in range(order_bits)]
    steps.append((8.5 * count_rounds + 15 + 8 * order_bits - 7.5, swap_most))
    for _, step in sorted(steps, key=lambda entry: entry[0]):
        step()
    last, state_sum = halves[count_rounds - 1].result()
    swap = cross(rows_of([last[block:], state_sum[fine:]]), pair_bits)
    final = S((block, inner), f32)
    d_w_inner, d_w_out, d_w_state = call(
        functools.partial(finish_kernel, count_rounds), [final, final, S((fine, 2 * state), f32)],
        [ids] + held["most"] + [last, state_sum, held["swap"], swap], "finish", limit=SMALL)
    d_tokens = held["tokens"]
    return d_tokens[None], d_w_inner, d_w_state, d_w_out


def solution(mesh):
    in_specs = (
        P("seq", "order", None),
        P("seq", "order", None),
        P("seq", "order"),
        P("seq", "order", "heads"),
        P(None, "heads"),
        P(),
        P(None, "heads"),
    )
    out_specs = (
        P("seq", "order", "heads"),
        P(("order", "seq"), "heads"),
        P(("order", "heads", "seq"), None),
        P(("order", "seq"), "heads"),
    )
    return jax.shard_map(
        per_device, mesh=mesh, in_specs=in_specs, out_specs=out_specs, check_vma=False
    )
```

```python
import functools

import jax
import jax.numpy as jnp
from jax import lax
from jax.experimental import pallas as pl
from jax.experimental.pallas import tpu as pltpu
from jax.sharding import PartitionSpec as P

CHUNK = 128
SHARES = (1, 1, 1, 1)
LIMIT = 24 * 1024 * 1024
LARGE = 60 * 1024 * 1024
HEAVY = 16_000_000_000
LIGHT = 16_000_000_000
SMALL = 16 * 1024 * 1024
f32 = jnp.float32
bf16 = jnp.bfloat16


def dot(a, b, ca=1, cb=0):
    return lax.dot_general(a, b, (((ca,), (cb,)), ((), ())), preferred_element_type=f32)


def log2(n):
    bits = n.bit_length() - 1
    assert 1 << bits == n
    return bits


def place(index, order):
    out = 0
    for rank, bit in enumerate(order):
        out = out + (((index >> bit) & 1) << (len(order) - 1 - rank))
    return out


def spread(values, first, heads, size):
    total = values.shape[0]
    row = lax.broadcasted_iota(jnp.int32, (total, heads * size), 0)
    col = lax.broadcasted_iota(jnp.int32, (total, heads * size), 1)
    low = (row - first) * size
    pick = jnp.where((col >= low) & (col < low + size), 1.0, 0.0).astype(bf16)
    high = values.astype(bf16)
    rest = values - high.astype(f32)
    middle = rest.astype(bf16)
    last = (rest - middle.astype(f32)).astype(bf16)
    return dot(high, pick, 0, 0) + dot(middle, pick, 0, 0) + dot(last, pick, 0, 0)


def triangle(upper):
    row = lax.broadcasted_iota(jnp.int32, (CHUNK, CHUNK), 0)
    col = lax.broadcasted_iota(jnp.int32, (CHUNK, CHUNK), 1)
    return row <= col if upper else row >= col


def one_hot_rows(offsets, rows):
    node = lax.broadcasted_iota(jnp.int32, (rows, offsets.shape[1]), 0)
    return jnp.where(node == offsets, 1.0, 0.0).astype(bf16)


def chunk_rows(cum_x, k):
    part = cum_x[k * CHUNK:(k + 1) * CHUNK]
    return part, part[CHUNK // 2 - 1:CHUNK // 2], part[CHUNK - 1:CHUNK]


def end_states(cum_x, x, dy, sc, sb, xs, ys, near):
    count = cum_x.shape[0] // CHUNK
    forward, back, decay = [], [], []
    for k in range(count):
        span = slice(k * CHUNK, (k + 1) * CHUNK)
        part, mid, last = chunk_rows(cum_x, k)
        x_s = (x[span] * jnp.exp(mid - part)).astype(bf16)
        y_s = (dy[span] * jnp.exp(part - mid)).astype(bf16)
        xs[span, :] = x_s
        ys[span, :] = y_s
        forward.append(jnp.exp(last - mid) * dot(sb[span, CHUNK:], x_s, 0, 0))
        back.append(jnp.exp(mid) * dot(sc[span, CHUNK:], y_s, 0, 0))
        decay.append(jnp.exp(last))
    run, run_back, factor = forward[0], back[-1], decay[0]
    for k in range(1, count):
        run = decay[k] * run + forward[k]
        factor = factor * decay[k]
        run_back = decay[count - 1 - k] * run_back + back[count - 1 - k]
    state = run.shape[0]
    near[:state, :] = run
    near[state:2 * state, :] = run_back
    near[2 * state:, :] = jnp.broadcast_to(factor, (8, factor.shape[1]))


def order_kernel(heads, size, ids, off, decays, *refs):
    sources, refs = refs[:5], refs[5:]
    outs = len(refs) // 2 - 3
    targets, refs = refs[:outs], refs[outs:]
    (tokens_v, cot_v, state_v, inner_v, out_v), refs = refs[:5], refs[5:]
    held, sems = refs[:outs], refs[outs]
    ordered, ordered_grad, early, sc, sb, cum = held[:6]
    cut = pl.ds(0, heads * size)
    sources = [*sources[:3], sources[3].at[:, cut], sources[4].at[:, cut]]
    loads = [pltpu.make_async_copy(source, target, sems.at[i])
             for i, (source, target) in enumerate(zip(sources, (tokens_v, cot_v, state_v, inner_v, out_v)))]
    stores = [pltpu.make_async_copy(source, target, sems.at[5 + i]) for i, (source, target) in enumerate(zip(held, targets))]
    for load in loads:
        load.start()
    base, role = ids[1], ids[4]
    rows = tokens_v.shape[0]
    hot = one_hot_rows(off[...] - base, rows)
    lower = triangle(False)
    upper = triangle(True)
    ones = jnp.where(upper, 1.0, 0.0)
    rates = jnp.log(decays[...])
    for k in range(rows // CHUNK):
        span = slice(k * CHUNK, (k + 1) * CHUNK)
        cum[:, span] = jnp.dot(rates[:, span], ones, precision=lax.Precision.HIGHEST, preferred_element_type=f32)
    stores[5].start()
    loads[0].wait()
    ordered[...] = dot(hot, tokens_v[...], 0, 0).astype(bf16)
    stores[0].start()
    loads[1].wait()
    ordered_grad[...] = dot(hot, cot_v[...], 0, 0).astype(bf16)
    stores[1].start()
    early[...] = jnp.where(role == 0, ordered_grad[...].astype(f32), ordered[...].astype(f32))
    stores[2].start()
    loads[2].wait()
    bc = dot(ordered[...], state_v[...]).astype(bf16)
    state = bc.shape[1] // 2
    for k in range(rows // CHUNK):
        span = slice(k * CHUNK, (k + 1) * CHUNK)
        b, c = bc[span, :state], bc[span, state:]
        sc[span, :CHUNK] = jnp.where(lower, dot(c, b, 1, 1), 0.0).astype(bf16)
        sc[span, CHUNK:] = c
        sb[span, :CHUNK] = jnp.where(upper, dot(b, c, 1, 1), 0.0).astype(bf16)
        sb[span, CHUNK:] = b
    stores[3].start()
    stores[4].start()
    loads[3].wait()
    x = dot(ordered[...], inner_v[...]).astype(bf16).astype(f32)
    loads[4].wait()
    dy = dot(ordered_grad[...], out_v[...]).astype(bf16).astype(f32)
    end_states(spread(cum[...], 0, heads, size), x, dy, sc, sb, *held[6:9])
    for store in stores[6:]:
        store.start()
    for store in stores:
        store.wait()


def rest_kernel(firsts, counts, size, sc, sb, cum, *refs):
    sources, refs = refs[:4], refs[4:]
    outs = len(refs) // 2 - 2
    targets, refs = refs[:outs], refs[outs:]
    (ordered, ordered_grad, inner_v, out_v), refs = refs[:4], refs[4:]
    held, sems = refs[:outs], refs[outs]
    base = firsts[0] * size
    cut = pl.ds(base, inner_v.shape[1])
    sources = [sources[0], sources[1], sources[2].at[:, cut], sources[3].at[:, cut]]
    loads = [pltpu.make_async_copy(source, target, sems.at[i])
             for i, (source, target) in enumerate(zip(sources, (ordered, ordered_grad, inner_v, out_v)))]
    stores = [pltpu.make_async_copy(source, target, sems.at[4 + i]) for i, (source, target) in enumerate(zip(held, targets))]
    for load in loads:
        load.start()
    for load in loads:
        load.wait()
    for r, (first, heads) in enumerate(zip(firsts, counts)):
        cut = slice(first * size - base, (first + heads) * size - base)
        x = dot(ordered[...], inner_v[:, cut]).astype(bf16).astype(f32)
        dy = dot(ordered_grad[...], out_v[:, cut]).astype(bf16).astype(f32)
        end_states(spread(cum[...], first, heads, size), x, dy, sc, sb, *held[3 * r:3 * r + 3])
        for store in stores[3 * r:3 * r + 3]:
            store.start()
    for store in stores:
        store.wait()


def join_kernel(ids, near, came, out):
    state = out.shape[0]
    lower, odd = ids[5] < 2, ids[5] & 1 == 1
    own = jnp.where(lower, near[:state, :], near[state:2 * state, :])
    other = jnp.where(lower, came[:state, :], came[state:2 * state, :])
    out[...] = jnp.where(odd == lower, own + near[2 * state:2 * state + 1, :] * other,
                         other + came[2 * state:2 * state + 1, :] * own)


def turn_kernel(orders, ids, ordered, ordered_grad, near, left):
    me, side, role = ids[0], ids[2], ids[4]
    rows, width = ordered.shape
    half = width // 2
    blocks = 1 << len(orders[0])
    size = width // blocks
    for part in range(2):
        span = slice(part * half, (part + 1) * half)
        own = jnp.where(role == 0, ordered[:, span].astype(f32), ordered_grad[:, span].astype(f32)).astype(bf16)
        value = jnp.concatenate([own.T, near[:, span].astype(bf16).T], axis=1)
        for block in range(blocks // 2):
            index = (block + part * (blocks // 2)) ^ me
            where = jnp.where(side == 0, place(index, orders[0]), place(index, orders[1]))
            left[pl.ds(pl.multiple_of(where * size, size), size), :] = value[block * size:(block + 1) * size]


def outputs_kernel(first, heads, size, pieces, ready, ids, xs, ys, sc, sb, cum, came, *refs):
    far = None if ready else refs[0]
    refs = refs if ready else refs[1:]
    owns, sends, (grad_x, grad_bc) = refs[:pieces], refs[pieces:2 * pieces], refs[2 * pieces:]
    cum_x = spread(cum[...], first, heads, size)
    count = cum_x.shape[0] // CHUNK
    lower = triangle(False)
    upper = triangle(True)
    role = ids[4]
    state = (came.shape[0] - 8) // 2
    before, after = came[:state, :], came[state:2 * state, :]
    if not ready:
        factor = came[2 * state:2 * state + 1, :]
        first_half, odd = ids[5] < 2, ids[5] & 1 == 1
        before, after = (
            jnp.where(odd, before + jnp.where(first_half, 0.0, factor * far[...]), jnp.where(first_half, 0.0, far[...])),
            jnp.where(odd, jnp.where(first_half, far[...], 0.0), after + jnp.where(first_half, factor * far[...], 0.0)))
    starts, afters = [before], [after]
    for k in range(count - 1):
        span = slice(k * CHUNK, (k + 1) * CHUNK)
        _, mid, last = chunk_rows(cum_x, k)
        starts.append(jnp.exp(last) * starts[-1] + jnp.exp(last - mid) * dot(sb[span, CHUNK:], xs[span, :], 0, 0))
    for k in range(count - 1, 0, -1):
        span = slice(k * CHUNK, (k + 1) * CHUNK)
        _, mid, last = chunk_rows(cum_x, k)
        afters.insert(0, jnp.exp(last) * afters[0] + jnp.exp(mid) * dot(sc[span, CHUNK:], ys[span, :], 0, 0))
    for k in range(count):
        span = slice(k * CHUNK, (k + 1) * CHUNK)
        part, mid, last = chunk_rows(cum_x, k)
        x_s, y_s = xs[span, :], ys[span, :]
        x_rows = jnp.concatenate([x_s, (starts[k] * jnp.exp(mid)).astype(bf16)], axis=0)
        y_rows = jnp.concatenate([y_s, (afters[k] * jnp.exp(last - mid)).astype(bf16)], axis=0)
        y = (jnp.exp(part - mid) * dot(sc[span, :], x_rows)).astype(bf16)
        dx = (jnp.exp(mid - part) * dot(sb[span, :], y_rows)).astype(bf16)
        grad_x[span, :] = dx
        y, dx = y.astype(f32), dx.astype(f32)
        for i, (own, send) in enumerate(zip(owns, sends)):
            cut = slice(i * own.shape[1], (i + 1) * own.shape[1])
            own[span, :] = jnp.where(role == 0, dx[:, cut], y[:, cut]).astype(bf16)
            send[span, :] = jnp.where(role == 0, y[:, cut], dx[:, cut])
        by_y = dot(y_s, x_rows, 1, 1)
        by_x = dot(x_s, y_rows, 1, 1)
        pairs = jnp.where(lower, by_y[:, :CHUNK], 0.0).astype(bf16)
        turned = jnp.where(upper, by_x[:, :CHUNK], 0.0).astype(bf16)
        grad_bc[span, :state] = dot(turned, sc[span, CHUNK:]) + by_x[:, CHUNK:]
        grad_bc[span, state:] = dot(pairs, sb[span, CHUNK:]) + by_y[:, CHUNK:]


def grads_kernel(left, own, came, keep, send):
    half = left.shape[0] // 2
    right = jnp.concatenate([own[...], came[...].astype(bf16)], axis=0)
    send[...] = dot(left[half:, :], right)
    keep[...] = dot(left[:half, :], right)


def back_kernel(rounds, s_orders, ids, *refs):
    grads, sums = refs[:rounds], refs[rounds:2 * rounds]
    w_inner, w_state, ordered, keep, state_keep, send, table = refs[2 * rounds:]
    side, me_state = ids[2], ids[3]
    grad_bc = sums[0][...]
    for part in sums[1:]:
        grad_bc = grad_bc + part[...]
    grad_bc = grad_bc.astype(bf16)
    width = ordered.shape[1]
    half = width // 2
    for out, which in ((send, 1 - side), (keep, side)):
        rows = pl.ds(pl.multiple_of(which * half, half), half)
        value = dot(grad_bc, w_state[rows, :], 1, 1)
        start = 0
        for part in grads:
            cols = part.shape[1]
            value = value + dot(part[...], w_inner[rows, start:start + cols], 1, 1)
            start += cols
        out[:, :half] = value
    fine = width >> len(s_orders[0])
    step = width // 4
    for quarter in range(4):
        value = dot(ordered[:, quarter * step:(quarter + 1) * step], grad_bc, 0, 0)
        for piece in range(step // fine):
            index = (quarter * step) // fine + piece
            index = index ^ me_state
            owner = side ^ ((index >> s_orders[0][0]) & 1)
            where = jnp.where(owner == 0, place(index, s_orders[0]), place(index, s_orders[1]))
            table[pl.ds(pl.multiple_of(where * fine, fine), fine), :] = value[piece * fine:(piece + 1) * fine]
    state_keep[...] = table[:half, :]
    send[:, half:] = table[half:, :]


def place_kernel(ids, off, keep, came, out):
    hot = one_hot_rows(off[...] - ids[1], out.shape[0])
    out[...] = dot(hot, (keep[...] + came[:, :keep.shape[1]]).astype(bf16)).astype(bf16)


def finish_kernel(rounds, ids, *refs):
    halves, (state, most, last, d_inner, d_out, d_state) = refs[:rounds], refs[rounds:]
    block, fine = d_inner.shape[0], d_state.shape[0]
    start = 0
    for r, half in enumerate(halves):
        cut = slice(start, start + half.shape[1])
        own, other = half[:block, :], most[:, cut] if r + 1 < rounds else last[:block, :]
        d_inner[:, cut] = jnp.where(ids[4] == 0, own, other)
        d_out[:, cut] = jnp.where(ids[4] == 0, other, own)
        start += half.shape[1]
    d_state[...] = state[:fine, :] + last[block:, :]


def flips(axis, bit):
    return [(i, i ^ (1 << bit)) for i in range(lax.axis_size(axis))]


def cross(value, bits):
    count = lax.axis_size("seq")
    pairs = [(h * count + s, h * count + (s ^ (1 << bit))) for h, bit in enumerate(bits) for s in range(count)]
    return lax.ppermute(value, ("heads", "seq"), pairs)


def total_of(parts, start, stop):
    out = parts[0][start:stop]
    for part in parts[1:]:
        out = out + part[start:stop]
    return out


def chain(near):
    count, mine = lax.axis_size("order"), lax.axis_index("order")
    state = (near.shape[0] - 8) // 2
    forward, back, total = near[:state], near[state:2 * state], near[2 * state:2 * state + 1]
    run, run_back = jnp.zeros_like(forward), jnp.zeros_like(back)
    for k in range(1, count):
        up = lax.ppermute(total * run + forward, "order", [(k - 1, k)])
        down = lax.ppermute(total * run_back + back, "order", [(count - k, count - k - 1)])
        run = jnp.where(mine == k, up, run)
        run_back = jnp.where(mine == count - k - 1, down, run_back)
    return jnp.concatenate([run, run_back, jnp.zeros_like(near[2 * state:])], axis=0)


class Line:
    def __init__(self, value):
        self.last = value

    def tie(self, *values):
        out = lax.optimization_barrier((self.last,) + values)
        self.last = out[0]
        return out[1:] if len(values) > 1 else out[1]

    def did(self, value):
        self.last = value


class Sum:
    def __init__(self, line, segments, hops):
        self.line, self.segments, self.hops = line, segments, list(hops)

    def hop(self):
        axis, bit = self.hops.pop(0)
        halves = [parts[0].shape[0] // 2 for parts in self.segments]
        flat = self.line.tie(*[part for parts in self.segments for part in parts])
        tied, start = [], 0
        for parts in self.segments:
            tied.append(flat[start:start + len(parts)])
            start += len(parts)
        message = rows_of([total_of(parts, half, 2 * half) for parts, half in zip(tied, halves)])
        self.line.did(message)
        came = lax.ppermute(message, axis, flips(axis, bit))
        start = 0
        self.segments = []
        for parts, half in zip(tied, halves):
            self.segments.append([p[:half] for p in parts] + [came[start:start + half]])
            start += half

    def result(self):
        return [total_of(parts, 0, parts[0].shape[0]) for parts in self.segments]


def rows_of(arrays):
    return arrays[0] if len(arrays) == 1 else jnp.concatenate(arrays, axis=0)


def whole(array):
    return pl.BlockSpec(array.shape, lambda *_: (0,) * len(array.shape))


def call(kernel, outs, args, name, scratch=(), specs=None, limit=LIMIT, out_specs=None, cost=LIGHT):
    specs = specs or {}
    out_specs = out_specs or {}
    in_specs = []
    for i, arg in enumerate(args):
        if i in specs:
            in_specs.append(specs[i])
        elif arg.dtype == jnp.int32 and arg.ndim == 1:
            in_specs.append(pl.BlockSpec(memory_space=pltpu.SMEM))
        else:
            in_specs.append(whole(arg))
    return pl.pallas_call(
        kernel,
        out_shape=tuple(outs),
        grid=(1,),
        in_specs=in_specs,
        out_specs=tuple(out_specs.get(i, whole(o)) for i, o in enumerate(outs)),
        scratch_shapes=list(scratch),
        compiler_params=pltpu.CompilerParams(vmem_limit_bytes=limit),
        cost_estimate=pl.CostEstimate(flops=cost, bytes_accessed=1000, transcendentals=0),
        name=name,
    )(*args)


def per_device(tokens, cotangent, node_order, decays, w_inner, w_state, w_out):
    assert tokens.shape[0] == 1
    tokens, cotangent, decays = tokens[0], cotangent[0], decays[0]
    rows, width = tokens.shape
    heads = decays.shape[1]
    inner = w_inner.shape[1]
    size = inner // heads
    state = w_state.shape[1] // 2
    unit = heads // sum(SHARES)
    firsts = [unit * sum(SHARES[:r]) for r in range(len(SHARES))]
    counts = [unit * share for share in SHARES]
    n_order, n_heads, n_seq = (lax.axis_size(a) for a in ("order", "heads", "seq"))
    o, h, s = (lax.axis_index(a) for a in ("order", "heads", "seq"))
    seq_bits, head_bits, order_bits = log2(n_seq), log2(n_heads), log2(n_order)
    assert seq_bits == 2 and head_bits == 1
    order_hops = [("order", b) for b in range(order_bits)]
    pair_bits, sum_bits = (0, 1), (1, 0)
    orders = [[sum_bits[c]] + [seq_bits + b for b in range(order_bits)] + [pair_bits[c]] for c in range(2)]
    s_orders = [[seq_bits, sum_bits[c]] + [seq_bits + 1 + b for b in range(order_bits)] + [pair_bits[c]] for c in range(2)]
    role = jnp.where(h == 0, s & 1, (s >> 1) & 1)
    ids = jnp.stack([o * n_seq + s, o * rows, h, (o * n_heads + h) * n_seq + s, role, o]).astype(jnp.int32)
    S = jax.ShapeDtypeStruct
    full = S((rows, width), bf16)
    sent = S((rows, width), f32)
    wide = S((rows, CHUNK + state), bf16)
    far_space = pl.BlockSpec(memory_space=pltpu.HBM)

    def ends(count):
        return [S((rows, count * size), bf16)] * 2 + [S((2 * state + 8, count * size), f32)]

    outs = [full, full, sent, wide, wide, S((heads, rows), f32)] + ends(counts[0])
    order_args = [ids, node_order, decays.T, tokens, cotangent, w_state, w_inner, w_out]
    cols = counts[0] * size
    made = call(
        functools.partial(order_kernel, counts[0], size), outs, order_args, "order",
        specs={i: far_space for i in range(3, 8)}, out_specs={i: far_space for i in range(len(outs))},
        scratch=[pltpu.VMEM(a.shape, a.dtype) for a in order_args[3:6]] + [pltpu.VMEM((width, cols), bf16)] * 2
        + [pltpu.VMEM(a.shape, a.dtype) for a in outs] + [pltpu.SemaphoreType.DMA((5 + len(outs),))],
        limit=LARGE, cost=HEAVY)
    ordered, ordered_grad, early, sc, sb, cum = made[:6]
    near_first = lax.ppermute(made[8], "order", flips("order", 0)) if n_order == 4 else chain(made[8])
    near_tokens = cross(early, pair_bits)
    outs = [out for count in counts[1:] for out in ends(count)]
    made += call(
        functools.partial(rest_kernel, firsts[1:], counts[1:], size), outs,
        [sc, sb, cum, ordered, ordered_grad, w_inner, w_out], "rest",
        specs={i: far_space for i in range(3, 7)}, out_specs={i: far_space for i in range(len(outs))},
        scratch=[pltpu.VMEM((rows, width), bf16)] * 2 + [pltpu.VMEM((width, inner - cols), bf16)] * 2
        + [pltpu.VMEM(a.shape, a.dtype) for a in outs] + [pltpu.SemaphoreType.DMA((4 + len(outs),))],
        limit=LARGE, cost=HEAVY)
    count_rounds = len(SHARES)
    block = width // (n_order * n_seq)
    fine = block // n_heads
    line = Line(ids)
    tree = n_order == 4
    nears = {0: near_first}
    line.did(made[11])
    incoming, owns, swapped, grads, sums, halves = {}, {}, {}, {}, {}, {}
    held = {}

    def join(r):
        near = made[8 + 3 * r]
        if tree:
            came = nears[r]
            joined, = call(join_kernel, [S((state, near.shape[1]), f32)], [line.tie(ids), near, came], f"join_{r}")
            line.did(joined)
            incoming[r] = (came, lax.ppermute(joined, "order", flips("order", 1)))
            if r + 1 < count_rounds:
                following, _ = lax.optimization_barrier((made[11 + 3 * r], joined))
                nears[r + 1] = lax.ppermute(following, "order", flips("order", 0))
        else:
            incoming[r] = (nears[r],)
            if r + 1 < count_rounds:
                nears[r + 1] = chain(made[11 + 3 * r])

    def outputs(r):
        cols = counts[r] * size
        own, send, grads[r], sums[r] = call(
            functools.partial(outputs_kernel, firsts[r], counts[r], size, 1, not tree),
            [S((rows, cols), bf16), S((rows, cols), f32), S((rows, cols), bf16), S((rows, 2 * state), f32)],
            [line.tie(ids), *made[6 + 3 * r:8 + 3 * r], sc, sb, cum, *incoming[r]], f"outputs_{r}", cost=HEAVY)
        line.did(send)
        owns[r], swapped[r] = own, cross(send, pair_bits)

    def turn():
        held["left"], = call(functools.partial(turn_kernel, orders), [S((width, 2 * rows), bf16)],
                             [line.tie(ids), ordered, ordered_grad, near_tokens], "turn")
        line.did(held["left"])

    def gradients(r):
        half = S((width // 2, counts[r] * size), f32)
        keep, send = call(grads_kernel, [half] * 2, [held["left"], line.tie(owns[r]), swapped[r]], f"grads_{r}")
        segments = [[keep]]
        if r == count_rounds - 1:
            whole_state = held["state"]
            middle = whole_state[0].shape[0] // 2
            send = rows_of([send, total_of(whole_state, middle, 2 * middle)])
            segments.append([part[:middle] for part in whole_state])
        line.did(send)
        came, start = cross(send, sum_bits), 0
        for parts in segments:
            parts.append(came[start:start + parts[0].shape[0]])
            start += parts[0].shape[0]
        halves[r] = Sum(line, segments, order_hops)

    def back():
        keep, state_keep, send = call(
            functools.partial(back_kernel, count_rounds, s_orders),
            [S((rows, width // 2), f32), S((width // 2, 2 * state), f32), S((rows, width // 2 + 2 * state), f32)],
            [line.tie(ids)] + [grads[r] for r in range(count_rounds)] + [sums[r] for r in range(count_rounds)]
            + [w_inner, w_state, ordered], "back", scratch=[pltpu.VMEM((width, 2 * state), f32)])
        line.did(send)
        held["keep"], held["came"] = keep, lax.ppermute(send, "heads", flips("heads", 0))
        held["state"] = [state_keep, held["came"][:, width // 2:]]

    def place_rows():
        held["tokens"], = call(place_kernel, [S((rows, width // 2), bf16)],
                               [line.tie(ids), node_order, held["keep"], held["came"]], "place")
        line.did(held["tokens"])

    done = {}

    def finish_round(r):
        halves[r].segments = [list(line.tie(*parts)) for parts in halves[r].segments]
        done[r], = halves[r].result()
        line.did(done[r])

    def swap_most():
        held["most"] = [done[r] for r in range(count_rounds - 1)]
        message = jnp.concatenate([line.tie(h)[block:] for h in held["most"]], axis=1)
        line.did(message)
        held["swap"] = cross(message, pair_bits)

    steps = [(-0.5, turn), (8.5 * count_rounds - 8, back), (8.5 * count_rounds + 1, place_rows)]
    for r in range(count_rounds):
        start = 8.5 * r
        steps += [(start - (9.5 if r < 2 else 8), functools.partial(join, r)), (start, functools.partial(outputs, r)),
                  (start + 11, functools.partial(gradients, r))]
        steps += [(start + 23 + 10 * k, lambda r=r: halves[r].hop()) for k in range(order_bits)]
        if r + 1 < count_rounds:
            steps.append((start + 23 + 10 * order_bits + 2, functools.partial(finish_round, r)))
    steps.append((8.5 * count_rounds + 15 + 10 * order_bits - 6.5, swap_most))
    for _, step in sorted(steps, key=lambda entry: entry[0]):
        step()
    last, state_sum = halves[count_rounds - 1].result()
    swap = cross(rows_of([last[block:], state_sum[fine:]]), pair_bits)
    final = S((block, inner), f32)
    d_w_inner, d_w_out, d_w_state = call(
        functools.partial(finish_kernel, count_rounds), [final, final, S((fine, 2 * state), f32)],
        [ids] + held["most"] + [last, state_sum, held["swap"], swap], "finish", limit=SMALL)
    d_tokens = held["tokens"]
    return d_tokens[None], d_w_inner, d_w_state, d_w_out


def solution(mesh):
    in_specs = (
        P("seq", "order", None),
        P("seq", "order", None),
        P("seq", "order"),
        P("seq", "order", "heads"),
        P(None, "heads"),
        P(),
        P(None, "heads"),
    )
    out_specs = (
        P("seq", "order", "heads"),
        P(("order", "seq"), "heads"),
        P(("order", "heads", "seq"), None),
        P(("order", "seq"), "heads"),
    )
    return jax.shard_map(
        per_device, mesh=mesh, in_specs=in_specs, out_specs=out_specs, check_vma=False
    )
```

```python
import functools

import jax
import jax.numpy as jnp
from jax import lax
from jax.experimental import pallas as pl
from jax.experimental.pallas import tpu as pltpu
from jax.sharding import PartitionSpec as P

CHUNK = 128
SHARES = (1, 1, 1, 1)
LIMIT = 24 * 1024 * 1024
LARGE = 60 * 1024 * 1024
HEAVY = 16_000_000_000
LIGHT = 16_000_000_000
SMALL = 16 * 1024 * 1024
f32 = jnp.float32
bf16 = jnp.bfloat16


def dot(a, b, ca=1, cb=0):
    return lax.dot_general(a, b, (((ca,), (cb,)), ((), ())), preferred_element_type=f32)


def log2(n):
    bits = n.bit_length() - 1
    assert 1 << bits == n
    return bits


def place(index, order):
    out = 0
    for rank, bit in enumerate(order):
        out = out + (((index >> bit) & 1) << (len(order) - 1 - rank))
    return out


def spread(values, first, heads, size):
    total = values.shape[0]
    row = lax.broadcasted_iota(jnp.int32, (total, heads * size), 0)
    col = lax.broadcasted_iota(jnp.int32, (total, heads * size), 1)
    low = (row - first) * size
    pick = jnp.where((col >= low) & (col < low + size), 1.0, 0.0).astype(bf16)
    high = values.astype(bf16)
    rest = values - high.astype(f32)
    middle = rest.astype(bf16)
    last = (rest - middle.astype(f32)).astype(bf16)
    return dot(high, pick, 0, 0) + dot(middle, pick, 0, 0) + dot(last, pick, 0, 0)


def triangle(upper):
    row = lax.broadcasted_iota(jnp.int32, (CHUNK, CHUNK), 0)
    col = lax.broadcasted_iota(jnp.int32, (CHUNK, CHUNK), 1)
    return row <= col if upper else row >= col


def one_hot_rows(offsets, rows):
    node = lax.broadcasted_iota(jnp.int32, (rows, offsets.shape[1]), 0)
    return jnp.where(node == offsets, 1.0, 0.0).astype(bf16)


def chunk_rows(cum_x, k):
    part = cum_x[k * CHUNK:(k + 1) * CHUNK]
    return part, part[CHUNK // 2 - 1:CHUNK // 2], part[CHUNK - 1:CHUNK]


def end_states(cum_x, x, dy, sc, sb, xs, ys, near):
    count = cum_x.shape[0] // CHUNK
    forward, back, decay = [], [], []
    for k in range(count):
        span = slice(k * CHUNK, (k + 1) * CHUNK)
        part, mid, last = chunk_rows(cum_x, k)
        x_s = (x[span] * jnp.exp(mid - part)).astype(bf16)
        y_s = (dy[span] * jnp.exp(part - mid)).astype(bf16)
        xs[span, :] = x_s
        ys[span, :] = y_s
        forward.append(jnp.exp(last - mid) * dot(sb[span, CHUNK:], x_s, 0, 0))
        back.append(jnp.exp(mid) * dot(sc[span, CHUNK:], y_s, 0, 0))
        decay.append(jnp.exp(last))
    run, run_back, factor = forward[0], back[-1], decay[0]
    for k in range(1, count):
        run = decay[k] * run + forward[k]
        factor = factor * decay[k]
        run_back = decay[count - 1 - k] * run_back + back[count - 1 - k]
    state = run.shape[0]
    near[:state, :] = run
    near[state:2 * state, :] = run_back
    near[2 * state:, :] = jnp.broadcast_to(factor, (8, factor.shape[1]))


def order_kernel(heads, size, ids, off, decays, *refs):
    sources, refs = refs[:5], refs[5:]
    outs = len(refs) // 2 - 3
    targets, refs = refs[:outs], refs[outs:]
    (tokens_v, cot_v, state_v, inner_v, out_v), refs = refs[:5], refs[5:]
    held, sems = refs[:outs], refs[outs]
    ordered, ordered_grad, early, sc, sb, cum = held[:6]
    cut = pl.ds(0, heads * size)
    sources = [*sources[:3], sources[3].at[:, cut], sources[4].at[:, cut]]
    loads = [pltpu.make_async_copy(source, target, sems.at[i])
             for i, (source, target) in enumerate(zip(sources, (tokens_v, cot_v, state_v, inner_v, out_v)))]
    stores = [pltpu.make_async_copy(source, target, sems.at[5 + i]) for i, (source, target) in enumerate(zip(held, targets))]
    for load in loads:
        load.start()
    base, role = ids[1], ids[4]
    rows = tokens_v.shape[0]
    hot = one_hot_rows(off[...] - base, rows)
    lower = triangle(False)
    upper = triangle(True)
    ones = jnp.where(upper, 1.0, 0.0)
    rates = jnp.log(decays[...])
    for k in range(rows // CHUNK):
        span = slice(k * CHUNK, (k + 1) * CHUNK)
        cum[:, span] = jnp.dot(rates[:, span], ones, precision=lax.Precision.HIGHEST, preferred_element_type=f32)
    stores[5].start()
    loads[0].wait()
    ordered[...] = dot(hot, tokens_v[...], 0, 0).astype(bf16)
    stores[0].start()
    loads[1].wait()
    ordered_grad[...] = dot(hot, cot_v[...], 0, 0).astype(bf16)
    stores[1].start()
    early[...] = jnp.where(role == 0, ordered_grad[...].astype(f32), ordered[...].astype(f32))
    stores[2].start()
    loads[2].wait()
    bc = dot(ordered[...], state_v[...]).astype(bf16)
    state = bc.shape[1] // 2
    for k in range(rows // CHUNK):
        span = slice(k * CHUNK, (k + 1) * CHUNK)
        b, c = bc[span, :state], bc[span, state:]
        sc[span, :CHUNK] = jnp.where(lower, dot(c, b, 1, 1), 0.0).astype(bf16)
        sc[span, CHUNK:] = c
        sb[span, :CHUNK] = jnp.where(upper, dot(b, c, 1, 1), 0.0).astype(bf16)
        sb[span, CHUNK:] = b
    stores[3].start()
    stores[4].start()
    loads[3].wait()
    x = dot(ordered[...], inner_v[...]).astype(bf16).astype(f32)
    loads[4].wait()
    dy = dot(ordered_grad[...], out_v[...]).astype(bf16).astype(f32)
    end_states(spread(cum[...], 0, heads, size), x, dy, sc, sb, *held[6:9])
    for store in stores[6:]:
        store.start()
    for store in stores:
        store.wait()


def rest_kernel(firsts, counts, size, sc, sb, cum, *refs):
    sources, refs = refs[:4], refs[4:]
    outs = len(refs) // 2 - 2
    targets, refs = refs[:outs], refs[outs:]
    (ordered, ordered_grad, inner_v, out_v), refs = refs[:4], refs[4:]
    held, sems = refs[:outs], refs[outs]
    base = firsts[0] * size
    cut = pl.ds(base, inner_v.shape[1])
    sources = [sources[0], sources[1], sources[2].at[:, cut], sources[3].at[:, cut]]
    loads = [pltpu.make_async_copy(source, target, sems.at[i])
             for i, (source, target) in enumerate(zip(sources, (ordered, ordered_grad, inner_v, out_v)))]
    stores = [pltpu.make_async_copy(source, target, sems.at[4 + i]) for i, (source, target) in enumerate(zip(held, targets))]
    for load in loads:
        load.start()
    for load in loads:
        load.wait()
    for r, (first, heads) in enumerate(zip(firsts, counts)):
        cut = slice(first * size - base, (first + heads) * size - base)
        x = dot(ordered[...], inner_v[:, cut]).astype(bf16).astype(f32)
        dy = dot(ordered_grad[...], out_v[:, cut]).astype(bf16).astype(f32)
        end_states(spread(cum[...], first, heads, size), x, dy, sc, sb, *held[3 * r:3 * r + 3])
        for store in stores[3 * r:3 * r + 3]:
            store.start()
    for store in stores:
        store.wait()


def join_kernel(ids, near, came, out):
    state = out.shape[0]
    lower, odd = ids[5] < 2, ids[5] & 1 == 1
    own = jnp.where(lower, near[:state, :], near[state:2 * state, :])
    other = jnp.where(lower, came[:state, :], came[state:2 * state, :])
    out[...] = jnp.where(odd == lower, own + near[2 * state:2 * state + 1, :] * other,
                         other + came[2 * state:2 * state + 1, :] * own)


def turn_kernel(orders, ids, ordered, ordered_grad, near, left):
    me, side, role = ids[0], ids[2], ids[4]
    rows, width = ordered.shape
    half = width // 2
    blocks = 1 << len(orders[0])
    size = width // blocks
    for part in range(2):
        span = slice(part * half, (part + 1) * half)
        own = jnp.where(role == 0, ordered[:, span].astype(f32), ordered_grad[:, span].astype(f32)).astype(bf16)
        value = jnp.concatenate([own.T, near[:, span].astype(bf16).T], axis=1)
        for block in range(blocks // 2):
            index = (block + part * (blocks // 2)) ^ me
            where = jnp.where(side == 0, place(index, orders[0]), place(index, orders[1]))
            left[pl.ds(pl.multiple_of(where * size, size), size), :] = value[block * size:(block + 1) * size]


def outputs_kernel(first, heads, size, pieces, ready, ids, xs, ys, sc, sb, cum, came, *refs):
    far = None if ready else refs[0]
    refs = refs if ready else refs[1:]
    owns, sends, (grad_x, grad_bc) = refs[:pieces], refs[pieces:2 * pieces], refs[2 * pieces:]
    cum_x = spread(cum[...], first, heads, size)
    count = cum_x.shape[0] // CHUNK
    lower = triangle(False)
    upper = triangle(True)
    role = ids[4]
    state = (came.shape[0] - 8) // 2
    before, after = came[:state, :], came[state:2 * state, :]
    if not ready:
        factor = came[2 * state:2 * state + 1, :]
        first_half, odd = ids[5] < 2, ids[5] & 1 == 1
        before, after = (
            jnp.where(odd, before + jnp.where(first_half, 0.0, factor * far[...]), jnp.where(first_half, 0.0, far[...])),
            jnp.where(odd, jnp.where(first_half, far[...], 0.0), after + jnp.where(first_half, factor * far[...], 0.0)))
    starts, afters = [before], [after]
    for k in range(count - 1):
        span = slice(k * CHUNK, (k + 1) * CHUNK)
        _, mid, last = chunk_rows(cum_x, k)
        starts.append(jnp.exp(last) * starts[-1] + jnp.exp(last - mid) * dot(sb[span, CHUNK:], xs[span, :], 0, 0))
    for k in range(count - 1, 0, -1):
        span = slice(k * CHUNK, (k + 1) * CHUNK)
        _, mid, last = chunk_rows(cum_x, k)
        afters.insert(0, jnp.exp(last) * afters[0] + jnp.exp(mid) * dot(sc[span, CHUNK:], ys[span, :], 0, 0))
    for k in range(count):
        span = slice(k * CHUNK, (k + 1) * CHUNK)
        part, mid, last = chunk_rows(cum_x, k)
        x_s, y_s = xs[span, :], ys[span, :]
        x_rows = jnp.concatenate([x_s, (starts[k] * jnp.exp(mid)).astype(bf16)], axis=0)
        y_rows = jnp.concatenate([y_s, (afters[k] * jnp.exp(last - mid)).astype(bf16)], axis=0)
        y = (jnp.exp(part - mid) * dot(sc[span, :], x_rows)).astype(bf16)
        dx = (jnp.exp(mid - part) * dot(sb[span, :], y_rows)).astype(bf16)
        grad_x[span, :] = dx
        y, dx = y.astype(f32), dx.astype(f32)
        for i, (own, send) in enumerate(zip(owns, sends)):
            cut = slice(i * own.shape[1], (i + 1) * own.shape[1])
            own[span, :] = jnp.where(role == 0, dx[:, cut], y[:, cut]).astype(bf16)
            send[span, :] = jnp.where(role == 0, y[:, cut], dx[:, cut])
        by_y = dot(y_s, x_rows, 1, 1)
        by_x = dot(x_s, y_rows, 1, 1)
        pairs = jnp.where(lower, by_y[:, :CHUNK], 0.0).astype(bf16)
        turned = jnp.where(upper, by_x[:, :CHUNK], 0.0).astype(bf16)
        grad_bc[span, :state] = dot(turned, sc[span, CHUNK:]) + by_x[:, CHUNK:]
        grad_bc[span, state:] = dot(pairs, sb[span, CHUNK:]) + by_y[:, CHUNK:]


def grads_kernel(left, own, came, keep, send):
    half = left.shape[0] // 2
    right = jnp.concatenate([own[...], came[...].astype(bf16)], axis=0)
    send[...] = dot(left[half:, :], right)
    keep[...] = dot(left[:half, :], right)


def back_kernel(rounds, s_orders, ids, *refs):
    grads, sums = refs[:rounds], refs[rounds:2 * rounds]
    w_inner, w_state, ordered, keep, state_keep, send, table = refs[2 * rounds:]
    side, me_state = ids[2], ids[3]
    grad_bc = sums[0][...]
    for part in sums[1:]:
        grad_bc = grad_bc + part[...]
    grad_bc = grad_bc.astype(bf16)
    width = ordered.shape[1]
    half = width // 2
    for out, which in ((send, 1 - side), (keep, side)):
        rows = pl.ds(pl.multiple_of(which * half, half), half)
        value = dot(grad_bc, w_state[rows, :], 1, 1)
        start = 0
        for part in grads:
            cols = part.shape[1]
            value = value + dot(part[...], w_inner[rows, start:start + cols], 1, 1)
            start += cols
        out[:, :half] = value
    fine = width >> len(s_orders[0])
    step = width // 4
    for quarter in range(4):
        value = dot(ordered[:, quarter * step:(quarter + 1) * step], grad_bc, 0, 0)
        for piece in range(step // fine):
            index = (quarter * step) // fine + piece
            index = index ^ me_state
            owner = side ^ ((index >> s_orders[0][0]) & 1)
            where = jnp.where(owner == 0, place(index, s_orders[0]), place(index, s_orders[1]))
            table[pl.ds(pl.multiple_of(where * fine, fine), fine), :] = value[piece * fine:(piece + 1) * fine]
    state_keep[...] = table[:half, :]
    send[:, half:] = table[half:, :]


def place_kernel(ids, off, keep, came, out):
    hot = one_hot_rows(off[...] - ids[1], out.shape[0])
    out[...] = dot(hot, (keep[...] + came[:, :keep.shape[1]]).astype(bf16)).astype(bf16)


def finish_kernel(rounds, ids, *refs):
    halves, (state, most, last, d_inner, d_out, d_state) = refs[:rounds], refs[rounds:]
    block, fine = d_inner.shape[0], d_state.shape[0]
    start = 0
    for r, half in enumerate(halves):
        cut = slice(start, start + half.shape[1])
        own, other = half[:block, :], most[:, cut] if r + 1 < rounds else last[:block, :]
        d_inner[:, cut] = jnp.where(ids[4] == 0, own, other)
        d_out[:, cut] = jnp.where(ids[4] == 0, other, own)
        start += half.shape[1]
    d_state[...] = state[:fine, :] + last[block:, :]


def flips(axis, bit):
    return [(i, i ^ (1 << bit)) for i in range(lax.axis_size(axis))]


def cross(value, bits):
    count = lax.axis_size("seq")
    pairs = [(h * count + s, h * count + (s ^ (1 << bit))) for h, bit in enumerate(bits) for s in range(count)]
    return lax.ppermute(value, ("heads", "seq"), pairs)


def total_of(parts, start, stop):
    out = parts[0][start:stop]
    for part in parts[1:]:
        out = out + part[start:stop]
    return out


def chain(near):
    count, mine = lax.axis_size("order"), lax.axis_index("order")
    state = (near.shape[0] - 8) // 2
    forward, back, total = near[:state], near[state:2 * state], near[2 * state:2 * state + 1]
    run, run_back = jnp.zeros_like(forward), jnp.zeros_like(back)
    for k in range(1, count):
        up = lax.ppermute(total * run + forward, "order", [(k - 1, k)])
        down = lax.ppermute(total * run_back + back, "order", [(count - k, count - k - 1)])
        run = jnp.where(mine == k, up, run)
        run_back = jnp.where(mine == count - k - 1, down, run_back)
    return jnp.concatenate([run, run_back, jnp.zeros_like(near[2 * state:])], axis=0)


class Line:
    def __init__(self, value):
        self.last = value

    def tie(self, *values):
        out = lax.optimization_barrier((self.last,) + values)
        self.last = out[0]
        return out[1:] if len(values) > 1 else out[1]

    def did(self, value):
        self.last = value


class Sum:
    def __init__(self, line, segments, hops):
        self.line, self.segments, self.hops = line, segments, list(hops)

    def hop(self):
        axis, bit = self.hops.pop(0)
        halves = [parts[0].shape[0] // 2 for parts in self.segments]
        flat = self.line.tie(*[part for parts in self.segments for part in parts])
        tied, start = [], 0
        for parts in self.segments:
            tied.append(flat[start:start + len(parts)])
            start += len(parts)
        message = rows_of([total_of(parts, half, 2 * half) for parts, half in zip(tied, halves)])
        self.line.did(message)
        came = lax.ppermute(message, axis, flips(axis, bit))
        start = 0
        self.segments = []
        for parts, half in zip(tied, halves):
            self.segments.append([p[:half] for p in parts] + [came[start:start + half]])
            start += half

    def result(self):
        return [total_of(parts, 0, parts[0].shape[0]) for parts in self.segments]


def rows_of(arrays):
    return arrays[0] if len(arrays) == 1 else jnp.concatenate(arrays, axis=0)


def whole(array):
    return pl.BlockSpec(array.shape, lambda *_: (0,) * len(array.shape))


def call(kernel, outs, args, name, scratch=(), specs=None, limit=LIMIT, out_specs=None, cost=LIGHT):
    specs = specs or {}
    out_specs = out_specs or {}
    in_specs = []
    for i, arg in enumerate(args):
        if i in specs:
            in_specs.append(specs[i])
        elif arg.dtype == jnp.int32 and arg.ndim == 1:
            in_specs.append(pl.BlockSpec(memory_space=pltpu.SMEM))
        else:
            in_specs.append(whole(arg))
    return pl.pallas_call(
        kernel,
        out_shape=tuple(outs),
        grid=(1,),
        in_specs=in_specs,
        out_specs=tuple(out_specs.get(i, whole(o)) for i, o in enumerate(outs)),
        scratch_shapes=list(scratch),
        compiler_params=pltpu.CompilerParams(vmem_limit_bytes=limit),
        cost_estimate=pl.CostEstimate(flops=cost, bytes_accessed=1000, transcendentals=0),
        name=name,
    )(*args)


def per_device(tokens, cotangent, node_order, decays, w_inner, w_state, w_out):
    assert tokens.shape[0] == 1
    tokens, cotangent, decays = tokens[0], cotangent[0], decays[0]
    rows, width = tokens.shape
    heads = decays.shape[1]
    inner = w_inner.shape[1]
    size = inner // heads
    state = w_state.shape[1] // 2
    unit = heads // sum(SHARES)
    firsts = [unit * sum(SHARES[:r]) for r in range(len(SHARES))]
    counts = [unit * share for share in SHARES]
    n_order, n_heads, n_seq = (lax.axis_size(a) for a in ("order", "heads", "seq"))
    o, h, s = (lax.axis_index(a) for a in ("order", "heads", "seq"))
    seq_bits, head_bits, order_bits = log2(n_seq), log2(n_heads), log2(n_order)
    assert seq_bits == 2 and head_bits == 1
    order_hops = [("order", b) for b in range(order_bits)]
    pair_bits, sum_bits = (0, 1), (1, 0)
    orders = [[sum_bits[c]] + [seq_bits + b for b in range(order_bits)] + [pair_bits[c]] for c in range(2)]
    s_orders = [[seq_bits, sum_bits[c]] + [seq_bits + 1 + b for b in range(order_bits)] + [pair_bits[c]] for c in range(2)]
    role = jnp.where(h == 0, s & 1, (s >> 1) & 1)
    ids = jnp.stack([o * n_seq + s, o * rows, h, (o * n_heads + h) * n_seq + s, role, o]).astype(jnp.int32)
    S = jax.ShapeDtypeStruct
    full = S((rows, width), bf16)
    sent = S((rows, width), f32)
    wide = S((rows, CHUNK + state), bf16)
    far_space = pl.BlockSpec(memory_space=pltpu.HBM)

    def ends(count):
        return [S((rows, count * size), bf16)] * 2 + [S((2 * state + 8, count * size), f32)]

    outs = [full, full, sent, wide, wide, S((heads, rows), f32)] + ends(counts[0])
    order_args = [ids, node_order, decays.T, tokens, cotangent, w_state, w_inner, w_out]
    cols = counts[0] * size
    made = call(
        functools.partial(order_kernel, counts[0], size), outs, order_args, "order",
        specs={i: far_space for i in range(3, 8)}, out_specs={i: far_space for i in range(len(outs))},
        scratch=[pltpu.VMEM(a.shape, a.dtype) for a in order_args[3:6]] + [pltpu.VMEM((width, cols), bf16)] * 2
        + [pltpu.VMEM(a.shape, a.dtype) for a in outs] + [pltpu.SemaphoreType.DMA((5 + len(outs),))],
        limit=LARGE, cost=HEAVY)
    ordered, ordered_grad, early, sc, sb, cum = made[:6]
    near_first = lax.ppermute(made[8], "order", flips("order", 0)) if n_order == 4 else chain(made[8])
    near_tokens = cross(early, pair_bits)
    outs = [out for count in counts[1:] for out in ends(count)]
    made += call(
        functools.partial(rest_kernel, firsts[1:], counts[1:], size), outs,
        [sc, sb, cum, ordered, ordered_grad, w_inner, w_out], "rest",
        specs={i: far_space for i in range(3, 7)}, out_specs={i: far_space for i in range(len(outs))},
        scratch=[pltpu.VMEM((rows, width), bf16)] * 2 + [pltpu.VMEM((width, inner - cols), bf16)] * 2
        + [pltpu.VMEM(a.shape, a.dtype) for a in outs] + [pltpu.SemaphoreType.DMA((4 + len(outs),))],
        limit=LARGE, cost=HEAVY)
    count_rounds = len(SHARES)
    block = width // (n_order * n_seq)
    fine = block // n_heads
    line = Line(ids)
    tree = n_order == 4
    nears = {0: near_first}
    line.did(made[11])
    incoming, owns, swapped, grads, sums, halves = {}, {}, {}, {}, {}, {}
    held = {}

    def join(r):
        near = made[8 + 3 * r]
        if tree:
            came = nears[r]
            joined, = call(join_kernel, [S((state, near.shape[1]), f32)], [line.tie(ids), near, came], f"join_{r}")
            line.did(joined)
            incoming[r] = (came, lax.ppermute(joined, "order", flips("order", 1)))
            if r + 1 < count_rounds:
                following, _ = lax.optimization_barrier((made[11 + 3 * r], joined))
                nears[r + 1] = lax.ppermute(following, "order", flips("order", 0))
        else:
            incoming[r] = (nears[r],)
            if r + 1 < count_rounds:
                nears[r + 1] = chain(made[11 + 3 * r])

    def outputs(r):
        cols = counts[r] * size
        own, send, grads[r], sums[r] = call(
            functools.partial(outputs_kernel, firsts[r], counts[r], size, 1, not tree),
            [S((rows, cols), bf16), S((rows, cols), f32), S((rows, cols), bf16), S((rows, 2 * state), f32)],
            [line.tie(ids), *made[6 + 3 * r:8 + 3 * r], sc, sb, cum, *incoming[r]], f"outputs_{r}", cost=HEAVY)
        line.did(send)
        owns[r], swapped[r] = own, cross(send, pair_bits)

    def turn():
        held["left"], = call(functools.partial(turn_kernel, orders), [S((width, 2 * rows), bf16)],
                             [line.tie(ids), ordered, ordered_grad, near_tokens], "turn")
        line.did(held["left"])

    def gradients(r):
        half = S((width // 2, counts[r] * size), f32)
        keep, send = call(grads_kernel, [half] * 2, [held["left"], line.tie(owns[r]), swapped[r]], f"grads_{r}")
        segments = [[keep]]
        if r == count_rounds - 1:
            whole_state = held["state"]
            middle = whole_state[0].shape[0] // 2
            send = rows_of([send, total_of(whole_state, middle, 2 * middle)])
            segments.append([part[:middle] for part in whole_state])
        line.did(send)
        came, start = cross(send, sum_bits), 0
        for parts in segments:
            parts.append(came[start:start + parts[0].shape[0]])
            start += parts[0].shape[0]
        halves[r] = Sum(line, segments, order_hops)

    def back():
        keep, state_keep, send = call(
            functools.partial(back_kernel, count_rounds, s_orders),
            [S((rows, width // 2), f32), S((width // 2, 2 * state), f32), S((rows, width // 2 + 2 * state), f32)],
            [line.tie(ids)] + [grads[r] for r in range(count_rounds)] + [sums[r] for r in range(count_rounds)]
            + [w_inner, w_state, ordered], "back", scratch=[pltpu.VMEM((width, 2 * state), f32)])
        line.did(send)
        held["keep"], held["came"] = keep, lax.ppermute(send, "heads", flips("heads", 0))
        held["state"] = [state_keep, held["came"][:, width // 2:]]

    def place_rows():
        held["tokens"], = call(place_kernel, [S((rows, width // 2), bf16)],
                               [line.tie(ids), node_order, held["keep"], held["came"]], "place")
        line.did(held["tokens"])

    done = {}

    def finish_round(r):
        halves[r].segments = [list(line.tie(*parts)) for parts in halves[r].segments]
        done[r], = halves[r].result()
        line.did(done[r])

    def swap_most():
        held["most"] = [done[r] for r in range(count_rounds - 1)]
        message = jnp.concatenate([line.tie(h)[block:] for h in held["most"]], axis=1)
        line.did(message)
        held["swap"] = cross(message, pair_bits)

    steps = [(-0.5, turn), (8.5 * count_rounds - 8, back), (8.5 * count_rounds + 3, place_rows)]
    for r in range(count_rounds):
        start = 8.5 * r
        steps += [(start - (9.5 if r < 2 else 8), functools.partial(join, r)), (start, functools.partial(outputs, r)),
                  (start + 11, functools.partial(gradients, r))]
        steps += [(start + 23 + 10 * k, lambda r=r: halves[r].hop()) for k in range(order_bits)]
        if r + 1 < count_rounds:
            steps.append((start + 23 + 10 * order_bits + 2, functools.partial(finish_round, r)))
    steps.append((8.5 * count_rounds + 15 + 10 * order_bits - 6.5, swap_most))
    for _, step in sorted(steps, key=lambda entry: entry[0]):
        step()
    last, state_sum = halves[count_rounds - 1].result()
    swap = cross(rows_of([last[block:], state_sum[fine:]]), pair_bits)
    final = S((block, inner), f32)
    d_w_inner, d_w_out, d_w_state = call(
        functools.partial(finish_kernel, count_rounds), [final, final, S((fine, 2 * state), f32)],
        [ids] + held["most"] + [last, state_sum, held["swap"], swap], "finish", limit=SMALL)
    d_tokens = held["tokens"]
    return d_tokens[None], d_w_inner, d_w_state, d_w_out


def solution(mesh):
    in_specs = (
        P("seq", "order", None),
        P("seq", "order", None),
        P("seq", "order"),
        P("seq", "order", "heads"),
        P(None, "heads"),
        P(),
        P(None, "heads"),
    )
    out_specs = (
        P("seq", "order", "heads"),
        P(("order", "seq"), "heads"),
        P(("order", "heads", "seq"), None),
        P(("order", "seq"), "heads"),
    )
    return jax.shard_map(
        per_device, mesh=mesh, in_specs=in_specs, out_specs=out_specs, check_vma=False
    )
```
